128 devices in a mesh: tx: 8 (over z, core), ty: 16 (over y, x).
Axes of the slice: x: 4, y: 4, z: 4, core: 2. Of those that a mesh axis runs over, the one named last changes fastest.
Arguments:
- adjoint_start: float32 [4, 4, 1024, 4096], P(None, None, 'tx', 'ty'), may hold values from -6 to 6
- mixing_h: float32 [4, 1024, 4096], P(None, 'tx', 'ty'), may hold values from 0.02 to 0.12
- mixing_v: float32 [3, 1024, 4096], P(None, 'tx', 'ty'), may hold values from 0.05 to 0.2
- courant: float32 [2, 4, 1024, 4096], P(None, None, 'tx', 'ty'), may hold values from -0.15 to 0.15
- coriolis: float32 [1024, 4096], P('tx', 'ty'), may hold values from -0.3 to 0.3
- misfit: float32 [2, 8, 524288], P(None, None, ('tx', 'ty')), may hold values from -6 to 6
- owner: int32 [2, 524288, 1], P(None, ('tx', 'ty')), may hold values from 0 to 127; in each aligned block of 4096 rows (0 to 4095, 4096 to 8191, ..., all dimensions but the last counted through in order) at most 64 rows name the same one
- column: int32 [2, 524288], P(None, ('tx', 'ty')), may hold values from 0 to 32767
Outputs:
- adjoint_end: float32 [4, 4, 1024, 4096], P(None, None, 'tx', 'ty')
The draws below stay inside these ranges and needn't reach their ends.
Inputs may be any that keep to these rules, and one draw needn't show every extreme that they name: `owner`: among the records of one device for one step, no tile is named more than 64 times, and in every draw some such block names one tile exactly 64 times.
All inputs are finite; a program needn't handle non-finite values.
Results may differ from the reference program's by a relative error of at most 0.0003.
Values sent between devices are 32-bit elements; how exact they have to be, the bound alone decides.
No kernel may reach another device: no remote copies, remote signals or barrier semaphores. Data moves between devices by JAX's collectives and lax.ppermute only.
A program may use at most 128 MiB of HBM per device.

```python
import math
import jax
import jax.numpy as jnp
import numpy as np

CA = 128
CB = 256
LEV = 4
STEPS = 2
CAP = 64
PROFS = 4096
RECORDS = 524288
NX = 1024
NY = 4096
N_TY = 16
DEVICES = 128


def place_ends(array, own_key, least, largest):
    shape = array.shape
    index_at = [jax.random.randint(jax.random.fold_in(own_key, axis), (), 0, shape[axis]) for axis in range(len(shape))]
    array = array.at[tuple(index_at)].set(least)
    longest = shape.index(max(shape))
    index_at[longest] = (index_at[longest] + 1) % shape[longest]
    return array.at[tuple(index_at)].set(largest)


def block_scale(key, dims, cuts, smallest, high):
    def one(position, blocks):
        draws = jax.random.uniform(jax.random.fold_in(jax.random.fold_in(key, 6), position), (blocks,), jnp.float32, smallest / len(cuts), high / len(cuts))
        return jnp.repeat(jnp.exp(draws), dims[position] // blocks).reshape((-1,) + (1,) * (len(dims) - position - 1))

    loudness = one(*cuts[0])
    for cut in cuts[1:]:
        loudness = loudness * one(*cut)
    return loudness


def routed_block(key, own, number, rows, count, top, limit, slope):
    sequence = jax.random.permutation(key, count)
    heavy_load, common = portions_of(count, rows * top, limit, slope, True), portions_of(count, rows * top, limit, slope, False)
    places = jnp.arange(count)

    def named(lengths, turn):
        used = int((lengths > 0).sum())
        fixed = max(1, used // 4)
        passed = fixed + (places - fixed + turn * (used - fixed)) % max(1, count - fixed)
        return jnp.zeros((count,), jnp.int32).at[sequence[jnp.where(places < fixed, places, passed)]].set(jnp.asarray(lengths, jnp.int32))

    lengths = jnp.where(number % 4 == 0, named(heavy_load, number // 4), named(common, number - number // 4 - 1))
    mixed = jax.random.permutation(jax.random.fold_in(own, 3), count)
    source_of, receiver = mixed[0:count // 2 * 2:2], mixed[1:count // 2 * 2:2]
    room = jnp.minimum(lengths[source_of] - 1, limit - lengths[receiver]) // 2
    room = jnp.where((source_of == sequence[0]) | (receiver == sequence[0]) | (lengths[receiver] == 0), 0, jnp.maximum(room, 0))
    passed = jax.random.randint(jax.random.fold_in(own, 4), (count // 2,), 0, 1 << 20) % (room + 1)
    lengths = lengths.at[source_of].add(-passed).at[receiver].add(passed)
    labels = jnp.searchsorted(jnp.cumsum(lengths), jnp.arange(rows * top), side="right").astype(jnp.int32)
    listing = labels.reshape(top, rows).T
    listing = listing[jax.random.permutation(jax.random.fold_in(own, 1), rows)]
    turn = jax.random.randint(jax.random.fold_in(own, 2), (rows, 1), 0, top)
    return jnp.take_along_axis(listing, (jnp.arange(top)[None, :] + turn) % top, axis=1)


def portions_of(number_of, total, reach, lean, full):
    loads = [(1 << 20) // math.isqrt(rank ** lean) + 1 for rank in range(1, number_of + 1)]
    largest = reach if full else min(reach, max(-(-total // number_of), total * loads[0] // sum(loads)))
    least = 1 if total - largest >= number_of - 1 else 0
    counts, spare = [largest] + [least] * (number_of - 1), total - largest - least * (number_of - 1)
    while spare > 0:
        movable = [i for i in range(1, number_of) if counts[i] < largest] or [i for i in range(1, number_of) if counts[i] < reach]
        pool, left = sum([loads[i] for i in movable]), spare
        for i in movable:
            extra = min(reach - counts[i], max(1, left * loads[i] // pool), spare)
            counts[i] = counts[i] + extra
            spare = spare - extra
    return np.array(counts)


def scatter_about(stream_key, shape, deviation, bound, shards=(), held_as=jnp.bfloat16):
    gain = block_scale(stream_key, shape, shards, -0.22, 0.18) if shards else 1.0
    values = jax.random.normal(stream_key, shape, jnp.float32) * deviation * gain
    return jnp.minimum(jnp.maximum(values, -bound), bound).astype(held_as)


def setup_inputs(seed: int = 0) -> dict:
    arg_keys = jax.random.split(jax.random.key(seed), 9)
    adjoint_start = scatter_about(arg_keys[0], (4, LEV, NX, NY), 1.0, 6.0, ((2, 8), (3, 16)), jnp.float32)
    mixing_h = jnp.clip(jnp.exp(math.log(0.12) - 1.7917595 * jax.random.uniform(arg_keys[1], (LEV, NX, NY), jnp.float32) ** block_scale(arg_keys[1], (LEV, NX, NY), ((1, 8), (2, 16)), -0.2, 0.2)), 0.02, 0.12)
    mixing_v = jnp.clip(jnp.exp(math.log(0.2) - 1.3862944 * jax.random.uniform(arg_keys[2], (LEV - 1, NX, NY), jnp.float32) ** block_scale(arg_keys[2], (LEV - 1, NX, NY), ((1, 8), (2, 16)), -0.2, 0.2)), 0.05, 0.2)
    courant = jnp.clip(jax.random.uniform(arg_keys[3], (2, LEV, NX, NY), jnp.float32, -0.15, 0.15) * block_scale(arg_keys[3], (2, LEV, NX, NY), ((2, 8), (3, 16)), -0.4, 0.0), -0.15, 0.15)
    coriolis = jnp.clip(jax.random.uniform(arg_keys[4], (NX, NY), jnp.float32, -0.3, 0.3) * block_scale(arg_keys[4], (NX, NY), ((0, 8), (1, 16)), -0.4, 0.0), -0.3, 0.3)
    misfit = scatter_about(arg_keys[5], (STEPS, 2 * LEV, RECORDS), 1.0, 6.0, ((2, 128),), jnp.float32)
    owner_keys = jax.random.split(jax.random.fold_in(arg_keys[6], 1), STEPS * RECORDS // PROFS)
    owner_turns = jax.random.permutation(jax.random.fold_in(arg_keys[6], 3), STEPS * RECORDS // PROFS)
    owner = jax.vmap(lambda own, number: routed_block(jax.random.fold_in(arg_keys[6], 2), own, number, PROFS, DEVICES, 1, CAP, 2))(owner_keys, owner_turns).reshape((STEPS, RECORDS, 1))
    column = place_ends(jax.random.randint(arg_keys[7], (STEPS, RECORDS), 0, CA * CB), jax.random.fold_in(arg_keys[7], 1), 0, (CA * CB) - 1).astype(jnp.int32)
    return {"adjoint_start": adjoint_start, "mixing_h": mixing_h, "mixing_v": mixing_v, "courant": courant, "coriolis": coriolis, "misfit": misfit, "owner": owner, "column": column}


def advance(padded, adjoint, mixing_h, mixing_v, courant, coriolis, forcing):
    upper_row = padded[:, :, 2:, 1:-1]
    lower_row = padded[:, :, :-2, 1:-1]
    right_col = padded[:, :, 1:-1, 2:]
    left_col = padded[:, :, 1:-1, :-2]
    laplacian = upper_row + lower_row + right_col + left_col - 4.0 * adjoint
    transport = 0.5 * courant[0] * (upper_row - lower_row) + 0.5 * courant[1] * (right_col - left_col)
    vertical_flux = mixing_v * (adjoint[:, 1:] - adjoint[:, :-1])
    vertical = jnp.pad(vertical_flux, ((0, 0), (0, 1), (0, 0), (0, 0))) - jnp.pad(vertical_flux, ((0, 0), (1, 0), (0, 0), (0, 0)))
    updated = adjoint + mixing_h * laplacian + transport + vertical
    rotation = coriolis * jnp.stack([adjoint[3], -adjoint[2]])
    return updated + jnp.concatenate([forcing, rotation], axis=0)


def forcing_of(values, owner, column):
    target = owner[:, 0]
    grid_row = (target // N_TY) * CA + column // CB
    grid_col = (target % N_TY) * CB + column % CB
    flat_index = (grid_row * NY + grid_col).astype(jnp.int32)
    summed = jnp.zeros((2 * LEV, NX * NY), jnp.float32).at[:, flat_index].add(values)
    return summed.reshape(2, LEV, NX, NY)


def reference(adjoint_start, mixing_h, mixing_v, courant, coriolis, misfit, owner, column):
    adjoint = adjoint_start
    for step_index in range(STEPS):
        forcing = forcing_of(misfit[step_index], owner[step_index], column[step_index])
        padded = jnp.pad(adjoint, ((0, 0), (0, 0), (1, 1), (1, 1)))
        adjoint = advance(padded, adjoint, mixing_h, mixing_v, courant, coriolis, forcing)
    return adjoint
```

```python
import functools
import jax
import jax.numpy as jnp
from jax import lax
from jax.experimental import pallas as pl
from jax.experimental.pallas import tpu as pltpu
from jax.sharding import PartitionSpec as P

CA, CB, LEV, STEPS, CAP = 128, 256, 4, 2, 64
VALS = 2 * LEV
WORDS = VALS + 1
CHUNK = 256
BF = jnp.bfloat16
NT = (((1,), (1,)), ((), ()))


def halves(x):
    top = x.astype(BF)
    return top, (x - top.astype(jnp.float32)).astype(BF)


def pack_kernel(devices, span, owner_ref, column_ref, misfit_ref, out_ref, acc_ref, place_ref):
    records = owner_ref.shape[2]
    groups = devices // 4
    r = lax.broadcasted_iota(jnp.int32, (CHUNK, CHUNK), 0)
    c = lax.broadcasted_iota(jnp.int32, (CHUNK, CHUNK), 1)
    earlier = (r < c).astype(jnp.float32).astype(BF)
    tiles = lax.broadcasted_iota(jnp.int32, (devices, CHUNK), 0)

    counts = [jnp.zeros((devices, 1), jnp.float32)] * STEPS
    for i in range(records // CHUNK):
        at = pl.ds(i * CHUNK, CHUNK)
        for t in range(STEPS):
            target = owner_ref[t, :, at]
            hot = tiles == target
            ones = hot.astype(jnp.float32)
            before = jnp.dot(ones.astype(BF), earlier, preferred_element_type=jnp.float32)
            slot = jnp.sum(jnp.where(hot, before + counts[t], 0.0), axis=0, keepdims=True)
            counts[t] = counts[t] + before[:, CHUNK - 1 :] + ones[:, CHUNK - 1 :]
            place_ref[t, :, at] = (target & 3) * CAP + slot.astype(jnp.int32)

    acc_ref[...] = jnp.zeros_like(acc_ref)
    group_row = lax.broadcasted_iota(jnp.int32, (groups, span), 0)
    place_row = lax.broadcasted_iota(jnp.int32, (CHUNK, span), 0)

    def body(i, carry):
        at = pl.ds(pl.multiple_of(i * span, span), span)
        for t in range(STEPS):
            group_hot = (group_row == (owner_ref[t, :, at] >> 2)).astype(jnp.float32).astype(BF)
            place_hot = (place_row == place_ref[t, :, at]).astype(jnp.float32).astype(BF)
            cell = column_ref[t : t + 1, at]
            high, low = halves(misfit_ref[t, :, at])
            row = (cell - (cell & (CB - 1))).astype(jnp.float32).astype(BF)
            col = ((cell & (CB - 1)) + 1).astype(jnp.float32).astype(BF)
            lhs_h = jnp.concatenate([group_hot * high[k : k + 1] for k in range(VALS)] + [group_hot * row], axis=0)
            lhs_l = jnp.concatenate([group_hot * low[k : k + 1] for k in range(VALS)] + [group_hot * col], axis=0)
            lhs = jnp.concatenate([lhs_h, lhs_l], axis=1)
            rhs = jnp.concatenate([place_hot, place_hot], axis=1)
            acc_ref[t] += lax.dot_general(lhs, rhs, NT, preferred_element_type=jnp.float32)
        return carry

    lax.fori_loop(0, records // span, body, 0)
    left = lax.broadcasted_iota(jnp.int32, (groups, 128), 1) < CAP
    for k in range(WORDS):
        for j in range(2):
            a = acc_ref[0, pl.ds(k * groups, groups), pl.ds(j * 128, 128)]
            b = acc_ref[1, pl.ds(k * groups, groups), pl.ds(j * 128, 128)]
            out_ref[pl.ds(2 * j * WORDS + k, groups, stride=4 * WORDS), :] = jnp.where(left, a, pltpu.roll(b, CAP, 1))
            out_ref[pl.ds((2 * j + 1) * WORDS + k, groups, stride=4 * WORDS), :] = jnp.where(left, pltpu.roll(a, CAP, 1), b)


def pack(owner, column, misfit, devices, span=512):
    return pl.pallas_call(
        functools.partial(pack_kernel, devices, span),
        out_shape=jax.ShapeDtypeStruct((devices * WORDS, 128), jnp.float32),
        in_specs=[pl.BlockSpec(memory_space=pltpu.VMEM)] * 3,
        out_specs=pl.BlockSpec(memory_space=pltpu.VMEM),
        scratch_shapes=[pltpu.VMEM((STEPS, WORDS * devices // 4, CHUNK), jnp.float32), pltpu.VMEM((STEPS, 1, 4096), jnp.int32)],
        compiler_params=pltpu.CompilerParams(vmem_limit_bytes=48 << 20),
        name="pack",
    )(owner, column, misfit)


def exchange(keys, span, reach):
    sub = lax.broadcasted_iota(jnp.int32, (8, 128), 0)
    count = len(keys)
    keys = list(keys)
    if reach < count:
        for v in range(count):
            w = v ^ reach
            if v > w:
                continue
            low, high = jnp.minimum(keys[v], keys[w]), jnp.maximum(keys[v], keys[w])
            if span < count:
                keys[v], keys[w] = (high, low) if v & span else (low, high)
            elif span < 8 * count:
                down = (sub & (span // count)) != 0
                keys[v], keys[w] = jnp.where(down, high, low), jnp.where(down, low, high)
            else:
                keys[v], keys[w] = low, high
        return keys
    step = reach // count
    upper = (sub & step) != 0
    if span < 8 * count:
        upper = upper != ((sub & (span // count)) != 0)
    for v in range(count):
        other = jnp.where((sub & step) != 0, pltpu.roll(keys[v], step, 0), pltpu.roll(keys[v], 8 - step, 0))
        keys[v] = jnp.where(upper, jnp.maximum(keys[v], other), jnp.minimum(keys[v], other))
    return keys


def sort_rows(keys):
    span = 2
    while span <= 8 * len(keys):
        reach = span // 2
        while reach:
            keys = exchange(keys, span, reach)
            reach //= 2
        span *= 2
    return keys


def order_kernel(got_ref, high_ref, low_ref, cell_ref):
    lanes = lax.broadcasted_iota(jnp.int32, (128, 128), 1)
    left = lanes < CAP

    def list_of(k):
        a = got_ref[pl.ds(k, 64, stride=WORDS), :]
        b = got_ref[pl.ds(64 * WORDS + k, 64, stride=WORDS), :]
        first = jnp.where(left[:64], a, pltpu.roll(b, CAP, 1))
        second = jnp.where(left[:64], pltpu.roll(a, CAP, 1), b)
        return jnp.concatenate([first, second], axis=0)

    ids = list_of(VALS).astype(jnp.int32)
    slot = lanes & (CAP - 1)
    spread = ((slot & 1) << 5) | ((slot & 2) << 3) | ((slot & 4) << 1) | ((slot & 8) >> 1) | ((slot & 16) >> 3) | ((slot & 32) >> 5)
    idle = ((spread << 1) | (lanes >> 6)) << 8
    key = (jnp.where(ids > 0, ids - 1, idle) << 7) | lanes
    turned = key.astype(jnp.float32).T
    keys = sort_rows([turned[8 * v : 8 * v + 8] for v in range(16)])
    keys = jnp.concatenate(keys, axis=0).astype(jnp.int32)
    source = (keys & 127).astype(jnp.float32).T.astype(jnp.int32)

    def place(ref, k, x):
        for v in range(0, 16, 2):
            a, b = x[8 * v : 8 * v + 8], x[8 * v + 8 : 8 * v + 16]
            g, h = v // 4, (v // 2) % 2
            l8 = left[:8]
            ref[0, k, pl.ds(8 * g, 8), pl.ds(128 * h, 128)] = jnp.where(l8, a, pltpu.roll(b, CAP, 1))
            ref[1, k, pl.ds(8 * g, 8), pl.ds(128 * h, 128)] = jnp.where(l8, pltpu.roll(a, CAP, 1), b)

    place(cell_ref, 0, (keys >> 7).astype(jnp.float32))
    for k in range(VALS):
        moved = jnp.take_along_axis(list_of(k), source, axis=1).T
        top = moved.astype(BF).astype(jnp.float32)
        place(high_ref, k, top)
        place(low_ref, k, moved - top)


def bounds_of(cell_ref, edge_ref):
    chunk = lax.broadcasted_iota(jnp.int32, (32, 128), 0)
    lane = lax.broadcasted_iota(jnp.int32, (32, 128), 1)
    lines = []
    for t in range(STEPS):
        row = cell_ref[t, 0].astype(jnp.int32) >> 8
        least = jnp.min(jnp.minimum(row[:, :128], row[:, 128:]).astype(jnp.float32), axis=1, keepdims=True)
        most = jnp.max(jnp.maximum(row[:, :128], row[:, 128:]).astype(jnp.float32), axis=1, keepdims=True)
        lines += [jnp.sum(jnp.where(chunk == lane, e, 0.0), axis=0, keepdims=True) for e in (least, most)]
    edge_ref[...] = jnp.concatenate(lines + [jnp.zeros((4, 128), jnp.float32)], axis=0).astype(jnp.int32)


def products(t, i, base, window, keep, high_ref, low_ref, cell_ref):
    row_iota = lax.broadcasted_iota(jnp.int32, (window, CHUNK), 0) + base
    col_iota = lax.broadcasted_iota(jnp.int32, (CB, CHUNK), 0)
    cell = cell_ref[t, 0, pl.ds(i, 1), :].astype(jnp.int32)
    col_hot = (col_iota == (cell & (CB - 1))).astype(jnp.float32).astype(BF)
    hit = row_iota == (cell >> 8)
    if keep is not None:
        hit = hit & (row_iota >= keep)
    row_hot = hit.astype(jnp.float32).astype(BF)
    lhs = jnp.concatenate([row_hot * ref[t, k, pl.ds(i, 1), :].astype(BF) for ref in (high_ref, low_ref) for k in range(VALS)], axis=0)
    out = lax.dot_general(lhs, col_hot, NT, preferred_element_type=jnp.float32)
    return out[: VALS * window] + out[VALS * window :]


def spread_step(t, window, unroll, high_ref, low_ref, cell_ref, edge_ref, acc_ref):
    def gain(base, out):
        for k in range(VALS):
            acc_ref[k, pl.ds(base, window), :] += out[k * window : (k + 1) * window]

    def first(i):
        return pl.multiple_of(jnp.minimum((edge_ref[2 * t, i] >> 3) << 3, CA - window), 8)

    def body(j, carry):
        chunks = [j * unroll + u for u in range(unroll)]
        bases = [first(i) for i in chunks]
        outs = [products(t, i, base, window, None, high_ref, low_ref, cell_ref) for i, base in zip(chunks, bases)]
        for base, out in zip(bases, outs):
            gain(base, out)
        return carry

    lax.fori_loop(0, 32 // unroll, body, 0)

    def rest(i, carry):
        def more(start):
            base = pl.multiple_of(jnp.minimum(start, CA - window), 8)
            gain(base, products(t, i, base, window, start, high_ref, low_ref, cell_ref))
            return start + window

        lax.while_loop(lambda start: start <= edge_ref[2 * t + 1, i], more, first(i) + window)
        return carry

    lax.fori_loop(0, 32, rest, 0)


FIELDS = 4
PLANES = FIELDS * LEV


def edge_lines(plane, top_ref, bottom_ref, left_ref, right_ref):
    lane = lax.broadcasted_iota(jnp.int32, (CA, 128), 1)
    picked = jnp.zeros((CA, 128), jnp.float32)
    for p in range(PLANES):
        top_ref[p : p + 1, :] = plane(p, pl.ds(0, 8), pl.ds(0, CB))[:1]
        bottom_ref[p : p + 1, :] = plane(p, pl.ds(CA - 8, 8), pl.ds(0, CB))[7:]
        picked = jnp.where(lane == p, plane(p, pl.ds(0, CA), pl.ds(0, 128))[:, :1], picked)
        picked = jnp.where(lane == PLANES + p, plane(p, pl.ds(0, CA), pl.ds(CB - 128, 128))[:, 127:], picked)
    lines = picked.T
    left_ref[...] = lines[:PLANES]
    right_ref[...] = lines[PLANES : 2 * PLANES]


EDGES = (
    jax.ShapeDtypeStruct((PLANES, CB), jnp.float32),
    jax.ShapeDtypeStruct((PLANES, CB), jnp.float32),
    jax.ShapeDtypeStruct((PLANES, CA), jnp.float32),
    jax.ShapeDtypeStruct((PLANES, CA), jnp.float32),
)
WHOLE = pl.BlockSpec(memory_space=pltpu.VMEM)
ANYWHERE = pl.BlockSpec(memory_space=pl.ANY)
PARAMS = pltpu.CompilerParams(vmem_limit_bytes=48 << 20)


def first_edges_kernel(state_ref, after_ref, *edge_refs):
    edge_lines(lambda p, rows, cols: state_ref[p, rows, cols], *edge_refs)


def first_edges(state, after):
    return pl.pallas_call(
        first_edges_kernel,
        out_shape=EDGES,
        in_specs=[WHOLE, ANYWHERE],
        out_specs=[WHOLE] * 4,
        compiler_params=PARAMS,
        name="first_edges",
    )(state, after)


def trade(edges):
    top, bottom, left, right = edges

    def moved(x, axis, forward):
        ends = lax.axis_size(axis) - 1
        pairs = [(i, i + 1) if forward else (i + 1, i) for i in range(ends)]
        return lax.ppermute(x, axis, pairs)

    return moved(bottom, "tx", True), moved(top, "tx", False), moved(right, "ty", True), moved(left, "ty", False)


def step_kernel(forced, ts_ref, uv_ref, before_ref, after_ref, prior_ref, next_ref, mix_h_ref, mix_v_ref, courant_ref, turn_ref, *rest):
    forcing_ref, out_ref, state_ref, column_ref, sem = rest if forced else (None, *rest)
    half = PLANES // 2
    loads = [
        pltpu.make_async_copy(ts_ref.at[pl.ds(0, half)], state_ref.at[pl.ds(0, half), pl.ds(8, CA)], sem.at[0]),
        pltpu.make_async_copy(uv_ref.at[pl.ds(half, half)], state_ref.at[pl.ds(half, half), pl.ds(8, CA)], sem.at[1]),
    ]
    for load in loads:
        load.start()
    for p in range(PLANES):
        state_ref[p, 0:8, :] = jnp.broadcast_to(before_ref[p : p + 1, :], (8, CB))
        state_ref[p, CA + 8 : CA + 16, :] = jnp.broadcast_to(after_ref[p : p + 1, :], (8, CB))
    column_ref[...] = jnp.concatenate([prior_ref[...], next_ref[...], jnp.zeros((128 - 2 * PLANES, CA), jnp.float32)], axis=0).T
    for load in loads:
        load.wait()
    sub = lax.broadcasted_iota(jnp.int32, (8, CB), 0)
    lane = lax.broadcasted_iota(jnp.int32, (8, CB), 1)

    def strip(i, carry):
        at = pl.multiple_of(i * 8, 8)
        rows = pl.ds(at, 8)
        sides = column_ref[rows, :]
        turn = turn_ref[rows, :]
        mix_v = [mix_v_ref[k, rows, :] for k in range(LEV - 1)]
        centre = [state_ref[p, pl.ds(at + 8, 8), :] for p in range(PLANES)]
        for k in range(LEV):
            mix_h = mix_h_ref[k, rows, :]
            c0 = 0.5 * courant_ref[0, k, rows, :]
            c1 = 0.5 * courant_ref[1, k, rows, :]
            for f in range(FIELDS):
                p = f * LEV + k
                a = centre[p]
                below = state_ref[p, rows, :]
                above = state_ref[p, pl.ds(at + 16, 8), :]
                up = jnp.where(sub == 7, pltpu.roll(above, 7, 0), pltpu.roll(a, 7, 0))
                down = jnp.where(sub == 0, pltpu.roll(below, 1, 0), pltpu.roll(a, 1, 0))
                right = jnp.where(lane == CB - 1, sides[:, PLANES + p : PLANES + p + 1], pltpu.roll(a, CB - 1, 1))
                left = jnp.where(lane == 0, sides[:, p : p + 1], pltpu.roll(a, 1, 1))
                new = a + mix_h * (up + down + right + left - 4.0 * a) + c0 * (up - down) + c1 * (right - left)
                if k < LEV - 1:
                    new = new + mix_v[k] * (centre[p + 1] - a)
                if k > 0:
                    new = new - mix_v[k - 1] * (a - centre[p - 1])
                if f == 2:
                    new = new + turn * centre[p + LEV]
                if f == 3:
                    new = new - turn * centre[p - LEV]
                if forced and f < 2:
                    new = new + forcing_ref[p, rows, :]
                out_ref[p, rows, :] = new
        return carry

    lax.fori_loop(0, CA // 8, strip, 0)


def step(ts, uv, halos, coefficients, forcing=None):
    extra = () if forcing is None else (forcing,)
    return pl.pallas_call(
        functools.partial(step_kernel, forcing is not None),
        out_shape=jax.ShapeDtypeStruct((PLANES, CA, CB), jnp.float32),
        in_specs=[ANYWHERE] * 2 + [WHOLE] * (8 + len(extra)),
        out_specs=WHOLE,
        scratch_shapes=[pltpu.VMEM((PLANES, CA + 16, CB), jnp.float32), pltpu.VMEM((CA, 128), jnp.float32), pltpu.SemaphoreType.DMA((2,))],
        compiler_params=PARAMS,
        name="advance",
    )(ts, uv, *halos, *coefficients, *extra)


LISTS = (
    jax.ShapeDtypeStruct((STEPS, VALS, 32, CHUNK), jnp.float32),
    jax.ShapeDtypeStruct((STEPS, VALS, 32, CHUNK), jnp.float32),
    jax.ShapeDtypeStruct((STEPS, 1, 32, CHUNK), jnp.float32),
    jax.ShapeDtypeStruct((8, 128), jnp.int32),
)
WINDOW, UNROLL = 40, 8


def first_records_kernel(got_ref, still_ref, ts_ref, high_ref, low_ref, cell_ref, edge_ref, top_ref, bottom_ref, left_ref, right_ref, smem_ref, sem):
    order_kernel(got_ref, high_ref, low_ref, cell_ref)
    bounds_of(cell_ref, edge_ref)
    copy = pltpu.make_async_copy(edge_ref, smem_ref, sem)
    copy.start()
    ts_ref[...] = still_ref[: PLANES // 2]
    copy.wait()
    spread_step(0, WINDOW, UNROLL, high_ref, low_ref, cell_ref, smem_ref, ts_ref)
    half = PLANES // 2
    edge_lines(lambda p, rows, cols: (ts_ref if p < half else still_ref)[p, rows, cols], top_ref, bottom_ref, left_ref, right_ref)


def first_records(got, still):
    out = pl.pallas_call(
        first_records_kernel,
        out_shape=(jax.ShapeDtypeStruct((PLANES // 2, CA, CB), jnp.float32),) + LISTS + EDGES,
        in_specs=[WHOLE] * 2,
        out_specs=[WHOLE] * 9,
        scratch_shapes=[pltpu.SMEM((8, 128), jnp.int32), pltpu.SemaphoreType.DMA(())],
        compiler_params=PARAMS,
        name="first_records",
    )(got, still)
    return out[0], out[1:5], out[5:]


def second_records_kernel(high_ref, low_ref, cell_ref, edge_ref, out_ref):
    out_ref[...] = jnp.zeros_like(out_ref)
    spread_step(1, WINDOW, UNROLL, high_ref, low_ref, cell_ref, edge_ref, out_ref)


def second_records(lists):
    return pl.pallas_call(
        second_records_kernel,
        out_shape=jax.ShapeDtypeStruct((PLANES // 2, CA, CB), jnp.float32),
        in_specs=[WHOLE] * 3 + [pl.BlockSpec(memory_space=pltpu.SMEM)],
        out_specs=WHOLE,
        compiler_params=PARAMS,
        name="second_records",
    )(*lists)


def local(adjoint_start, mixing_h, mixing_v, courant, coriolis, misfit, owner, column):
    devices = lax.axis_size("tx") * lax.axis_size("ty")
    state = adjoint_start.reshape(PLANES, CA, CB)
    coefficients = (mixing_h, mixing_v, courant, coriolis)
    sent = pack(owner.transpose(0, 2, 1), column, misfit, devices, 1024)
    got = lax.all_to_all(sent.reshape(devices, 1, WORDS * 128), ("tx", "ty"), split_axis=0, concat_axis=0, tiled=True)
    still = step(state, state, trade(first_edges(state, sent)), coefficients)
    ts, lists, edges = first_records(got.reshape(devices * WORDS, 128), still)
    halos = trade(edges)
    forcing = second_records(lists)
    return step(ts, still, halos, coefficients, forcing).reshape(FIELDS, LEV, CA, CB)


def solution(mesh):
    return jax.shard_map(
        local,
        mesh=mesh,
        in_specs=(
            P(None, None, "tx", "ty"),
            P(None, "tx", "ty"),
            P(None, "tx", "ty"),
            P(None, None, "tx", "ty"),
            P("tx", "ty"),
            P(None, None, ("tx", "ty")),
            P(None, ("tx", "ty"), None),
            P(None, ("tx", "ty")),
        ),
        out_specs=P(None, None, "tx", "ty"),
        check_vma=False,
    )
```

```python
import functools
import jax
import jax.numpy as jnp
from jax import lax
from jax.experimental import pallas as pl
from jax.experimental.pallas import tpu as pltpu
from jax.sharding import PartitionSpec as P

CA, CB, LEV, STEPS, CAP = 128, 256, 4, 2, 64
VALS = 2 * LEV
WORDS = VALS + 1
CHUNK = 256
BF = jnp.bfloat16
NT = (((1,), (1,)), ((), ()))
WHOLE = pl.BlockSpec(memory_space=pltpu.VMEM)
ANYWHERE = pl.BlockSpec(memory_space=pl.ANY)
PARAMS = pltpu.CompilerParams(vmem_limit_bytes=48 << 20)


def halves(x):
    top = x.astype(BF)
    return top, (x - top.astype(jnp.float32)).astype(BF)


def slots_kernel(devices, owner_ref, place_ref):
    r = lax.broadcasted_iota(jnp.int32, (CHUNK, CHUNK), 0)
    c = lax.broadcasted_iota(jnp.int32, (CHUNK, CHUNK), 1)
    earlier = (r < c).astype(jnp.float32).astype(BF)
    tiles = lax.broadcasted_iota(jnp.int32, (devices, CHUNK), 0)
    counts = [jnp.zeros((devices, 1), jnp.float32)] * STEPS
    for i in range(owner_ref.shape[2] // CHUNK):
        at = pl.ds(i * CHUNK, CHUNK)
        for t in range(STEPS):
            target = owner_ref[t, :, at]
            hot = tiles == target
            ones = hot.astype(jnp.float32)
            before = jnp.dot(ones.astype(BF), earlier, preferred_element_type=jnp.float32)
            slot = jnp.sum(jnp.where(hot, before + counts[t], 0.0), axis=0, keepdims=True)
            counts[t] = counts[t] + before[:, CHUNK - 1 :] + ones[:, CHUNK - 1 :]
            place_ref[t, :, at] = (target & 3) * CAP + slot.astype(jnp.int32)


def slots(owner, devices):
    return pl.pallas_call(
        functools.partial(slots_kernel, devices),
        out_shape=jax.ShapeDtypeStruct(owner.shape, jnp.int32),
        in_specs=[WHOLE],
        out_specs=WHOLE,
        compiler_params=PARAMS,
        name="slots",
    )(owner)


def gather_step(t, span, owner_ref, place_ref, column_ref, misfit_ref, acc_ref):
    groups = acc_ref.shape[0] // WORDS
    group_row = lax.broadcasted_iota(jnp.int32, (groups, span), 0)
    place_row = lax.broadcasted_iota(jnp.int32, (CHUNK, span), 0)

    def part(i):
        at = pl.ds(pl.multiple_of(i * span, span), span)
        group_hot = (group_row == (owner_ref[t, :, at] >> 2)).astype(jnp.float32).astype(BF)
        place_hot = (place_row == place_ref[t, :, at]).astype(jnp.float32).astype(BF)
        cell = column_ref[t : t + 1, at]
        high, low = halves(misfit_ref[t, :, at])
        row = (cell - (cell & (CB - 1))).astype(jnp.float32).astype(BF)
        col = ((cell & (CB - 1)) + 1).astype(jnp.float32).astype(BF)
        lhs_h = jnp.concatenate([group_hot * high[k : k + 1] for k in range(VALS)] + [group_hot * row], axis=0)
        lhs_l = jnp.concatenate([group_hot * low[k : k + 1] for k in range(VALS)] + [group_hot * col], axis=0)
        lhs = jnp.concatenate([lhs_h, lhs_l], axis=1)
        rhs = jnp.concatenate([place_hot, place_hot], axis=1)
        return lax.dot_general(lhs, rhs, NT, preferred_element_type=jnp.float32)

    acc_ref[...] = part(0)

    def body(i, carry):
        acc_ref[...] += part(i)
        return carry

    lax.fori_loop(1, owner_ref.shape[2] // span, body, 0)


def gather_first_kernel(span, owner_ref, place_ref, column_ref, misfit_ref, out_ref):
    gather_step(0, span, owner_ref, place_ref, column_ref, misfit_ref, out_ref)


def gather_second_kernel(span, owner_ref, place_ref, column_ref, misfit_ref, first_ref, out_ref, acc_ref):
    gather_step(1, span, owner_ref, place_ref, column_ref, misfit_ref, acc_ref)
    groups = acc_ref.shape[0] // WORDS
    left = lax.broadcasted_iota(jnp.int32, (groups, 128), 1) < CAP
    for k in range(WORDS):
        for j in range(2):
            a = first_ref[pl.ds(k * groups, groups), pl.ds(j * 128, 128)]
            b = acc_ref[pl.ds(k * groups, groups), pl.ds(j * 128, 128)]
            out_ref[pl.ds(2 * j * WORDS + k, groups, stride=4 * WORDS), :] = jnp.where(left, a, pltpu.roll(b, CAP, 1))
            out_ref[pl.ds((2 * j + 1) * WORDS + k, groups, stride=4 * WORDS), :] = jnp.where(left, pltpu.roll(a, CAP, 1), b)


def gather(records, devices, first=None, span=1024):
    rows = WORDS * devices // 4
    if first is None:
        kernel, shape, extra, scratch, name = gather_first_kernel, (rows, CHUNK), (), [], "gather_first"
    else:
        kernel, shape, extra, name = gather_second_kernel, (devices * WORDS, 128), (first,), "gather_second"
        scratch = [pltpu.VMEM((rows, CHUNK), jnp.float32)]
    return pl.pallas_call(
        functools.partial(kernel, span),
        out_shape=jax.ShapeDtypeStruct(shape, jnp.float32),
        in_specs=[WHOLE] * (4 + len(extra)),
        out_specs=WHOLE,
        scratch_shapes=scratch,
        compiler_params=PARAMS,
        name=name,
    )(*records, *extra)


def exchange(keys, span, reach):
    sub = lax.broadcasted_iota(jnp.int32, (8, 128), 0)
    count = len(keys)
    keys = list(keys)
    if reach < count:
        for v in range(count):
            w = v ^ reach
            if v > w:
                continue
            low, high = jnp.minimum(keys[v], keys[w]), jnp.maximum(keys[v], keys[w])
            if span < count:
                keys[v], keys[w] = (high, low) if v & span else (low, high)
            elif span < 8 * count:
                down = (sub & (span // count)) != 0
                keys[v], keys[w] = jnp.where(down, high, low), jnp.where(down, low, high)
            else:
                keys[v], keys[w] = low, high
        return keys
    step = reach // count
    upper = (sub & step) != 0
    if span < 8 * count:
        upper = upper != ((sub & (span // count)) != 0)
    for v in range(count):
        other = jnp.where((sub & step) != 0, pltpu.roll(keys[v], step, 0), pltpu.roll(keys[v], 8 - step, 0))
        keys[v] = jnp.where(upper, jnp.maximum(keys[v], other), jnp.minimum(keys[v], other))
    return keys


def sort_rows(keys):
    span = 2
    while span <= 8 * len(keys):
        reach = span // 2
        while reach:
            keys = exchange(keys, span, reach)
            reach //= 2
        span *= 2
    return keys


def order_kernel(got_ref, high_ref, low_ref, cell_ref):
    lanes = lax.broadcasted_iota(jnp.int32, (128, 128), 1)
    left = lanes < CAP

    def list_of(k):
        a = got_ref[pl.ds(k, 64, stride=WORDS), :]
        b = got_ref[pl.ds(64 * WORDS + k, 64, stride=WORDS), :]
        first = jnp.where(left[:64], a, pltpu.roll(b, CAP, 1))
        second = jnp.where(left[:64], pltpu.roll(a, CAP, 1), b)
        return jnp.concatenate([first, second], axis=0)

    ids = list_of(VALS).astype(jnp.int32)
    slot = lanes & (CAP - 1)
    spread = ((slot & 1) << 5) | ((slot & 2) << 3) | ((slot & 4) << 1) | ((slot & 8) >> 1) | ((slot & 16) >> 3) | ((slot & 32) >> 5)
    idle = ((spread << 1) | (lanes >> 6)) << 8
    key = (jnp.where(ids > 0, ids - 1, idle) << 7) | lanes
    turned = key.astype(jnp.float32).T
    keys = sort_rows([turned[8 * v : 8 * v + 8] for v in range(16)])
    keys = jnp.concatenate(keys, axis=0).astype(jnp.int32)
    source = (keys & 127).astype(jnp.float32).T.astype(jnp.int32)

    def place(ref, k, x):
        for v in range(0, 16, 2):
            a, b = x[8 * v : 8 * v + 8], x[8 * v + 8 : 8 * v + 16]
            g, h = v // 4, (v // 2) % 2
            l8 = left[:8]
            ref[0, k, pl.ds(8 * g, 8), pl.ds(128 * h, 128)] = jnp.where(l8, a, pltpu.roll(b, CAP, 1))
            ref[1, k, pl.ds(8 * g, 8), pl.ds(128 * h, 128)] = jnp.where(l8, pltpu.roll(a, CAP, 1), b)

    place(cell_ref, 0, (keys >> 7).astype(jnp.float32))
    for k in range(VALS):
        moved = jnp.take_along_axis(list_of(k), source, axis=1).T
        top = moved.astype(BF).astype(jnp.float32)
        place(high_ref, k, top)
        place(low_ref, k, moved - top)


def bounds_of(cell_ref, edge_ref):
    chunk = lax.broadcasted_iota(jnp.int32, (32, 128), 0)
    lane = lax.broadcasted_iota(jnp.int32, (32, 128), 1)
    lines = []
    for t in range(STEPS):
        row = cell_ref[t, 0].astype(jnp.int32) >> 8
        least = jnp.min(jnp.minimum(row[:, :128], row[:, 128:]).astype(jnp.float32), axis=1, keepdims=True)
        most = jnp.max(jnp.maximum(row[:, :128], row[:, 128:]).astype(jnp.float32), axis=1, keepdims=True)
        lines += [jnp.sum(jnp.where(chunk == lane, e, 0.0), axis=0, keepdims=True) for e in (least, most)]
    edge_ref[...] = jnp.concatenate(lines + [jnp.zeros((4, 128), jnp.float32)], axis=0).astype(jnp.int32)


def products(t, i, base, window, keep, high_ref, low_ref, cell_ref):
    row_iota = lax.broadcasted_iota(jnp.int32, (window, CHUNK), 0) + base
    col_iota = lax.broadcasted_iota(jnp.int32, (CB, CHUNK), 0)
    cell = cell_ref[t, 0, pl.ds(i, 1), :].astype(jnp.int32)
    col_hot = (col_iota == (cell & (CB - 1))).astype(jnp.float32).astype(BF)
    hit = row_iota == (cell >> 8)
    if keep is not None:
        hit = hit & (row_iota >= keep)
    row_hot = hit.astype(jnp.float32).astype(BF)
    lhs = jnp.concatenate([row_hot * ref[t, k, pl.ds(i, 1), :].astype(BF) for ref in (high_ref, low_ref) for k in range(VALS)], axis=0)
    out = lax.dot_general(lhs, col_hot, NT, preferred_element_type=jnp.float32)
    return out[: VALS * window] + out[VALS * window :]


def spread_step(t, chunks_from, chunks_to, window, unroll, high_ref, low_ref, cell_ref, edge_ref, acc_ref):
    def gain(base, out):
        for k in range(VALS):
            acc_ref[k, pl.ds(base, window), :] += out[k * window : (k + 1) * window]

    def first(i):
        return pl.multiple_of(jnp.minimum((edge_ref[2 * t, i] >> 3) << 3, CA - window), 8)

    def body(j, carry):
        chunks = [j * unroll + u for u in range(unroll)]
        bases = [first(i) for i in chunks]
        outs = [products(t, i, base, window, None, high_ref, low_ref, cell_ref) for i, base in zip(chunks, bases)]
        for base, out in zip(bases, outs):
            gain(base, out)
        return carry

    lax.fori_loop(chunks_from // unroll, chunks_to // unroll, body, 0)

    def rest(i, carry):
        def more(start):
            base = pl.multiple_of(jnp.minimum(start, CA - window), 8)
            gain(base, products(t, i, base, window, start, high_ref, low_ref, cell_ref))
            return start + window

        lax.while_loop(lambda start: start <= edge_ref[2 * t + 1, i], more, first(i) + window)
        return carry

    lax.fori_loop(chunks_from, chunks_to, rest, 0)


FIELDS = 4
PLANES = FIELDS * LEV


def edge_lines(plane, top_ref, bottom_ref, left_ref, right_ref):
    lane = lax.broadcasted_iota(jnp.int32, (CA, 128), 1)
    picked = jnp.zeros((CA, 128), jnp.float32)
    for p in range(PLANES):
        top_ref[p : p + 1, :] = plane(p, pl.ds(0, 8), pl.ds(0, CB))[:1]
        bottom_ref[p : p + 1, :] = plane(p, pl.ds(CA - 8, 8), pl.ds(0, CB))[7:]
        picked = jnp.where(lane == p, plane(p, pl.ds(0, CA), pl.ds(0, 128))[:, :1], picked)
        picked = jnp.where(lane == PLANES + p, plane(p, pl.ds(0, CA), pl.ds(CB - 128, 128))[:, 127:], picked)
    lines = picked.T
    left_ref[...] = lines[:PLANES]
    right_ref[...] = lines[PLANES : 2 * PLANES]


EDGES = (
    jax.ShapeDtypeStruct((PLANES, CB), jnp.float32),
    jax.ShapeDtypeStruct((PLANES, CB), jnp.float32),
    jax.ShapeDtypeStruct((PLANES, CA), jnp.float32),
    jax.ShapeDtypeStruct((PLANES, CA), jnp.float32),
)


def first_edges_kernel(state_ref, *edge_refs):
    edge_lines(lambda p, rows, cols: state_ref[p, rows, cols], *edge_refs)


def first_edges(state):
    return pl.pallas_call(
        first_edges_kernel,
        out_shape=EDGES,
        in_specs=[WHOLE],
        out_specs=[WHOLE] * 4,
        compiler_params=PARAMS,
        name="first_edges",
    )(state)


def moved(x, axis, forward):
    count = lax.axis_size(axis)
    pairs = [(i, (i + 1) % count) if forward else ((i + 1) % count, i) for i in range(count)]
    return lax.ppermute(x, axis, pairs)


def after(x, *others):
    return lax.optimization_barrier((x, *others))


def step_kernel(forced, ts_ref, uv_ref, before_ref, after_ref, prior_ref, next_ref, mix_h_ref, mix_v_ref, courant_ref, turn_ref, *rest):
    forcing_ref, out_ref, state_ref, column_ref, sem = rest if forced else (None, *rest)
    half = PLANES // 2
    loads = [
        pltpu.make_async_copy(ts_ref.at[pl.ds(0, half)], state_ref.at[pl.ds(0, half), pl.ds(8, CA)], sem.at[0]),
        pltpu.make_async_copy(uv_ref.at[pl.ds(half, half)], state_ref.at[pl.ds(half, half), pl.ds(8, CA)], sem.at[1]),
    ]
    for load in loads:
        load.start()
    tx, ty = lax.axis_index("tx"), lax.axis_index("ty")

    def inside(ref, there):
        return jnp.where(there, ref[...], 0.0)

    before = inside(before_ref, tx > 0)
    after = inside(after_ref, tx < lax.axis_size("tx") - 1)
    for p in range(PLANES):
        state_ref[p, 0:8, :] = jnp.broadcast_to(before[p : p + 1, :], (8, CB))
        state_ref[p, CA + 8 : CA + 16, :] = jnp.broadcast_to(after[p : p + 1, :], (8, CB))
    sides = [inside(prior_ref, ty > 0), inside(next_ref, ty < lax.axis_size("ty") - 1)]
    column_ref[...] = jnp.concatenate(sides + [jnp.zeros((128 - 2 * PLANES, CA), jnp.float32)], axis=0).T
    for load in loads:
        load.wait()
    sub = lax.broadcasted_iota(jnp.int32, (8, CB), 0)
    lane = lax.broadcasted_iota(jnp.int32, (8, CB), 1)

    def strip(i, carry):
        at = pl.multiple_of(i * 8, 8)
        rows = pl.ds(at, 8)
        sides = column_ref[rows, :]
        turn = turn_ref[rows, :]
        mix_v = [mix_v_ref[k, rows, :] for k in range(LEV - 1)]
        centre = [state_ref[p, pl.ds(at + 8, 8), :] for p in range(PLANES)]
        for k in range(LEV):
            mix_h = mix_h_ref[k, rows, :]
            c0 = 0.5 * courant_ref[0, k, rows, :]
            c1 = 0.5 * courant_ref[1, k, rows, :]
            for f in range(FIELDS):
                p = f * LEV + k
                a = centre[p]
                below = state_ref[p, rows, :]
                above = state_ref[p, pl.ds(at + 16, 8), :]
                up = jnp.where(sub == 7, pltpu.roll(above, 7, 0), pltpu.roll(a, 7, 0))
                down = jnp.where(sub == 0, pltpu.roll(below, 1, 0), pltpu.roll(a, 1, 0))
                right = jnp.where(lane == CB - 1, sides[:, PLANES + p : PLANES + p + 1], pltpu.roll(a, CB - 1, 1))
                left = jnp.where(lane == 0, sides[:, p : p + 1], pltpu.roll(a, 1, 1))
                new = a + mix_h * (up + down + right + left - 4.0 * a) + c0 * (up - down) + c1 * (right - left)
                if k < LEV - 1:
                    new = new + mix_v[k] * (centre[p + 1] - a)
                if k > 0:
                    new = new - mix_v[k - 1] * (a - centre[p - 1])
                if f == 2:
                    new = new + turn * centre[p + LEV]
                if f == 3:
                    new = new - turn * centre[p - LEV]
                if forced and f < 2:
                    new = new + forcing_ref[p, rows, :]
                out_ref[p, rows, :] = new
        return carry

    lax.fori_loop(0, CA // 8, strip, 0)


def step(ts, uv, halos, coefficients, forcing=None):
    extra = () if forcing is None else (forcing,)
    return pl.pallas_call(
        functools.partial(step_kernel, forcing is not None),
        out_shape=jax.ShapeDtypeStruct((PLANES, CA, CB), jnp.float32),
        in_specs=[ANYWHERE] * 2 + [WHOLE] * (8 + len(extra)),
        out_specs=WHOLE,
        scratch_shapes=[pltpu.VMEM((PLANES, CA + 16, CB), jnp.float32), pltpu.VMEM((CA, 128), jnp.float32), pltpu.SemaphoreType.DMA((2,))],
        compiler_params=PARAMS,
        name="advance",
    )(ts, uv, *halos, *coefficients, *extra)


LISTS = (
    jax.ShapeDtypeStruct((STEPS, VALS, 32, CHUNK), jnp.float32),
    jax.ShapeDtypeStruct((STEPS, VALS, 32, CHUNK), jnp.float32),
    jax.ShapeDtypeStruct((STEPS, 1, 32, CHUNK), jnp.float32),
    jax.ShapeDtypeStruct((8, 128), jnp.int32),
)
WINDOW, UNROLL = 40, 8


def first_records_kernel(got_ref, still_ref, ts_ref, high_ref, low_ref, cell_ref, edge_ref, top_ref, bottom_ref, left_ref, right_ref, smem_ref, sem):
    order_kernel(got_ref, high_ref, low_ref, cell_ref)
    bounds_of(cell_ref, edge_ref)
    copy = pltpu.make_async_copy(edge_ref, smem_ref, sem)
    copy.start()
    ts_ref[...] = still_ref[: PLANES // 2]
    copy.wait()
    spread_step(0, 0, 32, WINDOW, UNROLL, high_ref, low_ref, cell_ref, smem_ref, ts_ref)
    half = PLANES // 2
    edge_lines(lambda p, rows, cols: (ts_ref if p < half else still_ref)[p, rows, cols], top_ref, bottom_ref, left_ref, right_ref)


def first_records(got, still):
    out = pl.pallas_call(
        first_records_kernel,
        out_shape=(jax.ShapeDtypeStruct((PLANES // 2, CA, CB), jnp.float32),) + LISTS + EDGES,
        in_specs=[WHOLE] * 2,
        out_specs=[WHOLE] * 9,
        scratch_shapes=[pltpu.SMEM((8, 128), jnp.int32), pltpu.SemaphoreType.DMA(())],
        compiler_params=PARAMS,
        name="first_records",
    )(got, still)
    return out[0], out[1:5], out[5:]


def second_records_kernel(part, high_ref, low_ref, cell_ref, edge_ref, *rest):
    out_ref = rest[-1]
    out_ref[...] = rest[0][...] if part else jnp.zeros_like(out_ref)
    spread_step(1, 16 * part, 16 * part + 16, WINDOW, UNROLL, high_ref, low_ref, cell_ref, edge_ref, out_ref)


def second_records(lists, part, earlier=()):
    return pl.pallas_call(
        functools.partial(second_records_kernel, part),
        out_shape=jax.ShapeDtypeStruct((PLANES // 2, CA, CB), jnp.float32),
        in_specs=[WHOLE] * 3 + [pl.BlockSpec(memory_space=pltpu.SMEM)] + [WHOLE] * len(earlier),
        out_specs=WHOLE,
        input_output_aliases={4: 0} if earlier else {},
        compiler_params=PARAMS,
        name="second_records",
    )(*lists, *earlier)


def local(adjoint_start, mixing_h, mixing_v, courant, coriolis, misfit, owner, column):
    devices = lax.axis_size("tx") * lax.axis_size("ty")
    state = adjoint_start.reshape(PLANES, CA, CB)
    coefficients = (mixing_h, mixing_v, courant, coriolis)
    owner = owner.transpose(0, 2, 1)
    top, bottom, left, right = first_edges(state)
    places = slots(owner, devices)
    right, places = after(right, places)
    prior = moved(right, "ty", True)
    records = (owner, places, column, misfit)
    first = gather(records, devices)
    left, top, bottom, first = after(left, top, bottom, first)
    next_ = moved(left, "ty", False)
    sent = gather(records, devices, first)
    top, bottom, sent = after(top, bottom, sent)
    halos = moved(bottom, "tx", True), moved(top, "tx", False), prior, next_
    got = lax.all_to_all(sent.reshape(devices, 1, WORDS * 128), ("tx", "ty"), split_axis=0, concat_axis=0, tiled=True)
    still = step(state, state, halos, coefficients)

    ts, lists, (top, bottom, left, right) = first_records(got.reshape(devices * WORDS, 128), still)
    before, after_ = moved(bottom, "tx", True), moved(top, "tx", False)
    prior = moved(right, "ty", True)
    forcing = second_records(lists, 0)
    left, forcing = after(left, forcing)
    next_ = moved(left, "ty", False)
    forcing = second_records(lists, 1, (forcing,))
    return step(ts, still, (before, after_, prior, next_), coefficients, forcing).reshape(FIELDS, LEV, CA, CB)


def solution(mesh):
    return jax.shard_map(
        local,
        mesh=mesh,
        in_specs=(
            P(None, None, "tx", "ty"),
            P(None, "tx", "ty"),
            P(None, "tx", "ty"),
            P(None, None, "tx", "ty"),
            P("tx", "ty"),
            P(None, None, ("tx", "ty")),
            P(None, ("tx", "ty"), None),
            P(None, ("tx", "ty")),
        ),
        out_specs=P(None, None, "tx", "ty"),
        check_vma=False,
    )
```

```python
import functools
import jax
import jax.numpy as jnp
from jax import lax
from jax.experimental import pallas as pl
from jax.experimental.pallas import tpu as pltpu
from jax.sharding import PartitionSpec as P

CA, CB, LEV, STEPS, CAP = 128, 256, 4, 2, 64
FIELDS = 4
PLANES = FIELDS * LEV
VALS = 2 * LEV
WORDS = VALS + 1
WIRE = WORDS + 1
CHUNK = 256
BF = jnp.bfloat16
NT = (((1,), (1,)), ((), ()))
LIMIT = 24
WHOLE = pl.BlockSpec(memory_space=pltpu.VMEM)
ANYWHERE = pl.BlockSpec(memory_space=pl.ANY)
PARAMS = pltpu.CompilerParams(vmem_limit_bytes=LIMIT << 20)
STEP = pltpu.CompilerParams(vmem_limit_bytes=40 << 20)
FULL = pltpu.CompilerParams(vmem_limit_bytes=63400000)


def halves(x):
    top = x.astype(BF)
    return top, (x - top.astype(jnp.float32)).astype(BF)


def slots(owner_ref, place_ref, devices):
    r = lax.broadcasted_iota(jnp.int32, (CHUNK, CHUNK), 0)
    c = lax.broadcasted_iota(jnp.int32, (CHUNK, CHUNK), 1)
    earlier = (r < c).astype(jnp.float32).astype(BF)
    tiles = lax.broadcasted_iota(jnp.int32, (devices, CHUNK), 0)
    counts = [jnp.zeros((devices, 1), jnp.float32)] * STEPS
    for i in range(owner_ref.shape[2] // CHUNK):
        at = pl.ds(i * CHUNK, CHUNK)
        for t in range(STEPS):
            target = owner_ref[t, :, at]
            hot = tiles == target
            ones = hot.astype(jnp.float32)
            before = jnp.dot(ones.astype(BF), earlier, preferred_element_type=jnp.float32)
            slot = jnp.sum(jnp.where(hot, before + counts[t], 0.0), axis=0, keepdims=True)
            counts[t] = counts[t] + before[:, CHUNK - 1 :] + ones[:, CHUNK - 1 :]
            place_ref[t, :, at] = (target & 3) * CAP + slot.astype(jnp.int32)


def gather(span, owner_ref, place_ref, column_ref, misfit_ref, acc_ref):
    groups = acc_ref.shape[1] // WORDS
    group_row = lax.broadcasted_iota(jnp.int32, (groups, span), 0)
    place_row = lax.broadcasted_iota(jnp.int32, (CHUNK, span), 0)

    def part(t, i):
        at = pl.ds(pl.multiple_of(i * span, span), span)
        group_hot = (group_row == (owner_ref[t, :, at] >> 2)).astype(jnp.float32).astype(BF)
        place_hot = (place_row == place_ref[t, :, at]).astype(jnp.float32).astype(BF)
        cell = column_ref[t : t + 1, at]
        high, low = halves(misfit_ref[t, :, at])
        row = (cell - (cell & (CB - 1))).astype(jnp.float32).astype(BF)
        col = ((cell & (CB - 1)) + 1).astype(jnp.float32).astype(BF)
        lhs_h = jnp.concatenate([group_hot * high[k : k + 1] for k in range(VALS)] + [group_hot * row], axis=0)
        lhs_l = jnp.concatenate([group_hot * low[k : k + 1] for k in range(VALS)] + [group_hot * col], axis=0)
        lhs = jnp.concatenate([lhs_h, lhs_l], axis=1)
        rhs = jnp.concatenate([place_hot, place_hot], axis=1)
        return lax.dot_general(lhs, rhs, NT, preferred_element_type=jnp.float32)

    def body(i, carry):
        for t in range(STEPS):
            acc_ref[t] += part(t, i)
        return carry

    for t in range(STEPS):
        acc_ref[t] = part(t, 0)
    lax.fori_loop(1, owner_ref.shape[2] // span, body, 0)


def corner_row(first, final):
    plane = lax.broadcasted_iota(jnp.int32, (PLANES, 128), 0)
    lane = lax.broadcasted_iota(jnp.int32, (PLANES, 128), 1)
    row = jnp.zeros((PLANES, 128), jnp.float32)
    for c, x in enumerate((first[:, :1], first[:, CB - 1 :], final[:, :1], final[:, CB - 1 :])):
        row = jnp.where(lane == plane + c * PLANES, x, row)
    return jnp.sum(row, axis=0, keepdims=True)


def pack_kernel(devices, span, owner_any, column_any, misfit_any, state_any, out_any, owner_ref, column_ref, misfit_ref, place_ref, acc_ref, out_ref, tile_ref, sem):
    pairs = [(owner_any, owner_ref), (column_any, column_ref), (misfit_any, misfit_ref)]
    pairs += [(state_any.at[:, pl.ds(at, 8)], tile_ref.at[n]) for n, at in enumerate((0, CA - 8))]
    loads = [pltpu.make_async_copy(x, y, sem.at[n]) for n, (x, y) in enumerate(pairs)]
    for load in loads:
        load.start()
    loads[0].wait()
    slots(owner_ref, place_ref, devices)
    for load in loads[1:]:
        load.wait()
    first = jnp.concatenate([tile_ref[0, p, :1, :] for p in range(PLANES)], axis=0)
    final = jnp.concatenate([tile_ref[1, p, 7:, :] for p in range(PLANES)], axis=0)
    out_ref[pl.ds(WORDS, devices, stride=WIRE), :] = jnp.broadcast_to(corner_row(first, final), (devices, 128))
    gather(span, owner_ref, place_ref, column_ref, misfit_ref, acc_ref)
    groups = devices // 4
    left = lax.broadcasted_iota(jnp.int32, (groups, 128), 1) < CAP
    for k in range(WORDS):
        for j in range(2):
            a = acc_ref[0, pl.ds(k * groups, groups), pl.ds(j * 128, 128)]
            b = acc_ref[1, pl.ds(k * groups, groups), pl.ds(j * 128, 128)]
            out_ref[pl.ds(2 * j * WIRE + k, groups, stride=4 * WIRE), :] = jnp.where(left, a, pltpu.roll(b, CAP, 1))
            out_ref[pl.ds((2 * j + 1) * WIRE + k, groups, stride=4 * WIRE), :] = jnp.where(left, pltpu.roll(a, CAP, 1), b)
    store = pltpu.make_async_copy(out_ref, out_any, sem.at[5])
    store.start()
    store.wait()


def pack(owner, column, misfit, state, devices, span=1024):
    sent = jax.ShapeDtypeStruct((devices * WIRE, 128), jnp.float32)
    return pl.pallas_call(
        functools.partial(pack_kernel, devices, span),
        out_shape=sent,
        in_specs=[ANYWHERE] * 4,
        out_specs=ANYWHERE,
        scratch_shapes=[
            pltpu.VMEM(owner.shape, jnp.int32),
            pltpu.VMEM(column.shape, jnp.int32),
            pltpu.VMEM(misfit.shape, jnp.float32),
            pltpu.VMEM(owner.shape, jnp.int32),
            pltpu.VMEM((STEPS, WORDS * devices // 4, CHUNK), jnp.float32),
            pltpu.VMEM(sent.shape, jnp.float32),
            pltpu.VMEM((2, PLANES, 8, CB), jnp.float32),
            pltpu.SemaphoreType.DMA((6,)),
        ],
        compiler_params=FULL,
        name="pack",
    )(owner, column, misfit, state)


def exchange(keys, span, reach):
    sub = lax.broadcasted_iota(jnp.int32, (8, 128), 0)
    count = len(keys)
    keys = list(keys)
    if reach < count:
        for v in range(count):
            w = v ^ reach
            if v > w:
                continue
            low, high = jnp.minimum(keys[v], keys[w]), jnp.maximum(keys[v], keys[w])
            if span < count:
                keys[v], keys[w] = (high, low) if v & span else (low, high)
            elif span < 8 * count:
                down = (sub & (span // count)) != 0
                keys[v], keys[w] = jnp.where(down, high, low), jnp.where(down, low, high)
            else:
                keys[v], keys[w] = low, high
        return keys
    step = reach // count
    upper = (sub & step) != 0
    if span < 8 * count:
        upper = upper != ((sub & (span // count)) != 0)
    for v in range(count):
        other = jnp.where((sub & step) != 0, pltpu.roll(keys[v], step, 0), pltpu.roll(keys[v], 8 - step, 0))
        keys[v] = jnp.where(upper, jnp.maximum(keys[v], other), jnp.minimum(keys[v], other))
    return keys


def sort_rows(keys):
    span = 2
    while span <= 8 * len(keys):
        reach = span // 2
        while reach:
            keys = exchange(keys, span, reach)
            reach //= 2
        span *= 2
    return keys


def order_kernel(got_ref, high_ref, low_ref, cell_ref):
    lanes = lax.broadcasted_iota(jnp.int32, (128, 128), 1)
    left = lanes < CAP

    def list_of(k):
        a = got_ref[pl.ds(k, 64, stride=WIRE), :]
        b = got_ref[pl.ds(64 * WIRE + k, 64, stride=WIRE), :]
        first = jnp.where(left[:64], a, pltpu.roll(b, CAP, 1))
        second = jnp.where(left[:64], pltpu.roll(a, CAP, 1), b)
        return jnp.concatenate([first, second], axis=0)

    ids = list_of(VALS).astype(jnp.int32)
    slot = lanes & (CAP - 1)
    spread = ((slot & 1) << 5) | ((slot & 2) << 3) | ((slot & 4) << 1) | ((slot & 8) >> 1) | ((slot & 16) >> 3) | ((slot & 32) >> 5)
    idle = ((spread << 1) | (lanes >> 6)) << 8
    key = (jnp.where(ids > 0, ids - 1, idle) << 7) | lanes
    turned = key.astype(jnp.float32).T
    keys = sort_rows([turned[8 * v : 8 * v + 8] for v in range(16)])
    keys = jnp.concatenate(keys, axis=0).astype(jnp.int32)
    source = (keys & 127).astype(jnp.float32).T.astype(jnp.int32)

    def place(ref, k, x):
        for v in range(0, 16, 2):
            a, b = x[8 * v : 8 * v + 8], x[8 * v + 8 : 8 * v + 16]
            g, h = v // 4, (v // 2) % 2
            l8 = left[:8]
            ref[0, k, pl.ds(8 * g, 8), pl.ds(128 * h, 128)] = jnp.where(l8, a, pltpu.roll(b, CAP, 1))
            ref[1, k, pl.ds(8 * g, 8), pl.ds(128 * h, 128)] = jnp.where(l8, pltpu.roll(a, CAP, 1), b)

    place(cell_ref, 0, (keys >> 7).astype(jnp.float32))
    for k in range(VALS):
        moved = jnp.take_along_axis(list_of(k), source, axis=1).T
        top = moved.astype(BF).astype(jnp.float32)
        place(high_ref, k, top)
        place(low_ref, k, moved - top)


def bounds_of(cell_ref, edge_ref):
    chunk = lax.broadcasted_iota(jnp.int32, (32, 128), 0)
    lane = lax.broadcasted_iota(jnp.int32, (32, 128), 1)
    lines = []
    for t in range(STEPS):
        row = cell_ref[t, 0].astype(jnp.int32) >> 8
        least = jnp.min(jnp.minimum(row[:, :128], row[:, 128:]).astype(jnp.float32), axis=1, keepdims=True)
        most = jnp.max(jnp.maximum(row[:, :128], row[:, 128:]).astype(jnp.float32), axis=1, keepdims=True)
        lines += [jnp.sum(jnp.where(chunk == lane, e, 0.0), axis=0, keepdims=True) for e in (least, most)]
    edge_ref[...] = jnp.concatenate(lines + [jnp.zeros((4, 128), jnp.float32)], axis=0).astype(jnp.int32)


def products(t, i, base, window, keep, high_ref, low_ref, cell_ref):
    row_iota = lax.broadcasted_iota(jnp.int32, (window, CHUNK), 0) + base
    col_iota = lax.broadcasted_iota(jnp.int32, (CB, CHUNK), 0)
    cell = cell_ref[t, 0, pl.ds(i, 1), :].astype(jnp.int32)
    col_hot = (col_iota == (cell & (CB - 1))).astype(jnp.float32).astype(BF)
    hit = row_iota == (cell >> 8)
    if keep is not None:
        hit = hit & (row_iota >= keep)
    row_hot = hit.astype(jnp.float32).astype(BF)
    lhs = jnp.concatenate([row_hot * ref[t, k, pl.ds(i, 1), :].astype(BF) for ref in (high_ref, low_ref) for k in range(VALS)], axis=0)
    out = lax.dot_general(lhs, col_hot, NT, preferred_element_type=jnp.float32)
    return out[: VALS * window] + out[VALS * window :]


def spread_step(t, chunks_from, chunks_to, window, unroll, high_ref, low_ref, cell_ref, edge_ref, acc_ref):
    def gain(base, out):
        for k in range(VALS):
            acc_ref[k, pl.ds(base, window), :] += out[k * window : (k + 1) * window]

    def first(i):
        return pl.multiple_of(jnp.minimum((edge_ref[2 * t, i] >> 3) << 3, CA - window), 8)

    def body(j, carry):
        chunks = [j * unroll + u for u in range(unroll)]
        bases = [first(i) for i in chunks]
        outs = [products(t, i, base, window, None, high_ref, low_ref, cell_ref) for i, base in zip(chunks, bases)]
        for base, out in zip(bases, outs):
            gain(base, out)
        return carry

    lax.fori_loop(chunks_from // unroll, chunks_to // unroll, body, 0)

    def rest(i, carry):
        def more(start):
            base = pl.multiple_of(jnp.minimum(start, CA - window), 8)
            gain(base, products(t, i, base, window, start, high_ref, low_ref, cell_ref))
            return start + window

        lax.while_loop(lambda start: start <= edge_ref[2 * t + 1, i], more, first(i) + window)
        return carry

    lax.fori_loop(chunks_from, chunks_to, rest, 0)


def row_lines(plane, count, top_ref, bottom_ref):
    for p in range(count):
        top_ref[p : p + 1, :] = plane(p, pl.ds(0, 8), pl.ds(0, CB))[:1]
        bottom_ref[p : p + 1, :] = plane(p, pl.ds(CA - 8, 8), pl.ds(0, CB))[7:]


def column_lines(plane, count):
    lane = lax.broadcasted_iota(jnp.int32, (CA, 128), 1)
    picked = jnp.zeros((CA, 128), jnp.float32)
    for p in range(count):
        picked = jnp.where(lane == p, plane(p, pl.ds(0, CA), pl.ds(0, 128))[:, :1], picked)
        picked = jnp.where(lane == count + p, plane(p, pl.ds(0, CA), pl.ds(CB - 128, 128))[:, 127:], picked)
    lines = picked.T
    return lines[:count], lines[count : 2 * count]


def moved(x, axis, forward):
    count = lax.axis_size(axis)
    pairs = [(i, (i + 1) % count) if forward else ((i + 1) % count, i) for i in range(count)]
    return lax.ppermute(x, axis, pairs)


def after(x, *others):
    return lax.optimization_barrier((x, *others))


FRAME = PLANES + 2 * LEV


def per_plane(levels):
    return jnp.concatenate([levels] * FIELDS, axis=0)


def inside(ref, there):
    return jnp.where(there, ref[...], 0.0)


def write_frame(plane, mix_h_ref, courant_ref, frame_ref):
    columns = column_lines(plane, PLANES)
    mix = column_lines(lambda k, rows, cols: mix_h_ref[k, rows, cols], LEV)
    along = column_lines(lambda k, rows, cols: courant_ref[0, k, rows, cols], LEV)
    across = column_lines(lambda k, rows, cols: courant_ref[1, k, rows, cols], LEV)
    place = lax.broadcasted_iota(jnp.int32, (LEV, CA), 1)
    for n, sign in ((0, -0.5), (1, 0.5)):
        ends = jnp.where(place == 0, mix[n] - 0.5 * along[n], jnp.where(place == CA - 1, mix[n] + 0.5 * along[n], 0.0))
        frame_ref[2 * FRAME :, n * CA : (n + 1) * CA] = jnp.concatenate([columns[n], mix[n] + sign * across[n], ends], axis=0)
    place = lax.broadcasted_iota(jnp.int32, (LEV, CB), 1)
    for n, sign, at in ((0, -0.5, 0), (1, 0.5, 7)):
        rows = pl.ds((CA - 8) * n, 8)

        def line(read, count):
            return jnp.concatenate([read(k, rows, pl.ds(0, CB))[at : at + 1] for k in range(count)], axis=0)

        mix = line(lambda k, rows, cols: mix_h_ref[k, rows, cols], LEV)
        along = line(lambda k, rows, cols: courant_ref[0, k, rows, cols], LEV)
        across = line(lambda k, rows, cols: courant_ref[1, k, rows, cols], LEV)
        ends = jnp.where(place == 0, mix - 0.5 * across, jnp.where(place == CB - 1, mix + 0.5 * across, 0.0))
        frame_ref[n * FRAME : (n + 1) * FRAME, :] = jnp.concatenate([line(plane, PLANES), mix + sign * along, ends], axis=0)


def ends_of(length, first, final):
    place = lax.broadcasted_iota(jnp.int32, (PLANES, length), 1)
    return jnp.where(place == 0, first, jnp.where(place == length - 1, final, 0.0))


def beside(sent, own, corners):
    edge, factor, ends = sent[:PLANES], sent[2 * PLANES : 2 * PLANES + LEV], sent[2 * PLANES + LEV :]
    return edge + per_plane(factor) * own[:PLANES] + per_plane(ends) * corners


def gained(sent, own):
    return per_plane(own[PLANES : PLANES + LEV]) * sent[PLANES : 2 * PLANES]


def step_kernel(last, *refs):
    half = PLANES // 2
    if last:
        ts_any, uv_any, mix_h_ref, mix_v_ref, courant_ref, turn_ref, *sent_refs, frame_ref, corner_ref, forcing_ref, out_any, state_ref, column_ref, out_ref, sem, out_sem = refs
        uv_any_half = uv_any
    else:
        ts_any, mix_h_any, mix_v_any, courant_any, turn_any, ts_out, uv_out, frame_any, edge_any = refs[:9]
        state_ref, mix_h_ref, mix_v_ref, courant_ref, turn_ref, frame_ref, edge_ref, out_ref, sem, out_sem = refs[9:]
        uv_any_half = ts_any.at[pl.ds(half, half)]
    pairs = [(ts_any.at[pl.ds(0, half)], state_ref.at[pl.ds(0, half), pl.ds(8, CA)]), (uv_any_half, state_ref.at[pl.ds(half, half), pl.ds(8, CA)])]
    if not last:
        pairs += [(mix_h_any, mix_h_ref), (mix_v_any, mix_v_ref), (courant_any, courant_ref), (turn_any, turn_ref)]
    loads = [pltpu.make_async_copy(x, y, sem.at[n]) for n, (x, y) in enumerate(pairs)]
    for load in loads:
        load.start()
    if last:
        tx, ty = lax.axis_index("tx"), lax.axis_index("ty")
        there = tx > 0, tx < lax.axis_size("tx") - 1, ty > 0, ty < lax.axis_size("ty") - 1
        before, after, prior, next_ = [inside(ref, flag) for ref, flag in zip(sent_refs, there)]
        top, bottom = frame_ref[:FRAME], frame_ref[FRAME : 2 * FRAME]
        left, right = frame_ref[2 * FRAME :, :CA], frame_ref[2 * FRAME :, CA:]
        corner = [corner_ref[:, c : c + 1] for c in range(4)]
        beside_prior = beside(prior, left, ends_of(CA, corner[3], corner[1]))
        beside_next = beside(next_, right, ends_of(CA, corner[2], corner[0]))
        spare = jnp.zeros((128 - 4 * PLANES, CA), jnp.float32)
        column_ref[...] = jnp.concatenate([beside_prior, beside_next, gained(prior, left), gained(next_, right), spare], axis=0).T
        beside_before = beside(before, top, ends_of(CB, corner[3], corner[2]))
        beside_after = beside(after, bottom, ends_of(CB, corner[1], corner[0]))
        gain_before, gain_after = gained(before, top), gained(after, bottom)
        for p in range(PLANES):
            state_ref[p, 0:8, :] = jnp.broadcast_to(beside_before[p : p + 1, :], (8, CB))
            state_ref[p, CA + 8 : CA + 16, :] = jnp.broadcast_to(beside_after[p : p + 1, :], (8, CB))
    else:
        state_ref[:, 0:8, :] = jnp.zeros((PLANES, 8, CB), jnp.float32)
        state_ref[:, CA + 8 : CA + 16, :] = jnp.zeros((PLANES, 8, CB), jnp.float32)
    for load in loads:
        load.wait()
    if last:
        edge = lax.broadcasted_iota(jnp.int32, (CA, 128), 1)
        for p in range(PLANES):
            for lanes, at, n in ((pl.ds(0, 128), 0, 2), (pl.ds(CB - 128, 128), 127, 3)):
                gain = column_ref[:, n * PLANES + p : n * PLANES + p + 1]
                state_ref[p, pl.ds(8, CA), lanes] += jnp.where(edge == at, gain, 0.0)
            state_ref[p, 8:9, :] += gain_before[p : p + 1, :]
            state_ref[p, CA + 7 : CA + 8, :] += gain_after[p : p + 1, :]
    else:
        write_frame(lambda p, rows, cols: state_ref[p, pl.ds(8 + rows.start, rows.size), cols], mix_h_ref, courant_ref, frame_ref)
        frame_store = pltpu.make_async_copy(frame_ref, frame_any, sem.at[6])
        frame_store.start()
    sub = lax.broadcasted_iota(jnp.int32, (8, CB), 0)
    lane = lax.broadcasted_iota(jnp.int32, (8, CB), 1)

    def store_of(i):
        rows = pl.ds(pl.multiple_of(i * 8, 8), 8)
        if last:
            return [pltpu.make_async_copy(out_ref.at[:, rows], out_any.at[:, rows], out_sem.at[0, i])]
        parts = (pl.ds(0, half), ts_out), (pl.ds(half, half), uv_out)
        return [pltpu.make_async_copy(out_ref.at[planes, rows], out.at[:, rows], out_sem.at[n, i]) for n, (planes, out) in enumerate(parts)]

    def strip(i, carry):
        at = pl.multiple_of(i * 8, 8)
        rows = pl.ds(at, 8)
        sides = column_ref[rows, :] if last else None
        turn = turn_ref[rows, :]
        mix_v = [mix_v_ref[k, rows, :] for k in range(LEV - 1)]
        centre = [state_ref[p, pl.ds(at + 8, 8), :] for p in range(PLANES)]
        for k in range(LEV):
            mix_h = mix_h_ref[k, rows, :]
            c0 = 0.5 * courant_ref[0, k, rows, :]
            c1 = 0.5 * courant_ref[1, k, rows, :]
            for f in range(FIELDS):
                p = f * LEV + k
                a = centre[p]
                below = state_ref[p, rows, :]
                above = state_ref[p, pl.ds(at + 16, 8), :]
                up = jnp.where(sub == 7, pltpu.roll(above, 7, 0), pltpu.roll(a, 7, 0))
                down = jnp.where(sub == 0, pltpu.roll(below, 1, 0), pltpu.roll(a, 1, 0))
                right = jnp.where(lane == CB - 1, sides[:, PLANES + p : PLANES + p + 1] if last else 0.0, pltpu.roll(a, CB - 1, 1))
                left = jnp.where(lane == 0, sides[:, p : p + 1] if last else 0.0, pltpu.roll(a, 1, 1))
                new = a + mix_h * (up + down + right + left - 4.0 * a) + c0 * (up - down) + c1 * (right - left)
                if k < LEV - 1:
                    new = new + mix_v[k] * (centre[p + 1] - a)
                if k > 0:
                    new = new - mix_v[k - 1] * (a - centre[p - 1])
                if f == 2:
                    new = new + turn * centre[p + LEV]
                if f == 3:
                    new = new - turn * centre[p - LEV]
                if last and f < 2:
                    new = new + forcing_ref[p, rows, :]
                out_ref[p, rows, :] = new
        for store in store_of(i):
            store.start()
        return carry

    def finish(i, carry):
        for store in store_of(i):
            store.wait()
        return carry

    lax.fori_loop(0, CA // 8, strip, 0)
    if not last:

        def plane(p, rows, cols):
            return out_ref[half + p, rows, cols]

        row_lines(plane, half, edge_ref.at[pl.ds(0, half)], edge_ref.at[pl.ds(half, half)])
        edge_ref[PLANES:, :CA], edge_ref[PLANES:, CA:] = column_lines(plane, half)
        edge_store = pltpu.make_async_copy(edge_ref, edge_any, sem.at[7])
        edge_store.start()
    lax.fori_loop(0, CA // 8, finish, 0)
    if not last:
        frame_store.wait()
        edge_store.wait()


HALF = jax.ShapeDtypeStruct((PLANES // 2, CA, CB), jnp.float32)


def first_step(state, coefficients):
    frame = jax.ShapeDtypeStruct((3 * FRAME, CB), jnp.float32)
    edge = jax.ShapeDtypeStruct((PLANES + PLANES // 2, CB), jnp.float32)
    scratch = [pltpu.VMEM((PLANES, CA + 16, CB), jnp.float32)] + [pltpu.VMEM(x.shape, jnp.float32) for x in (*coefficients, frame, edge)]
    scratch += [pltpu.VMEM((PLANES, CA, CB), jnp.float32), pltpu.SemaphoreType.DMA((8,)), pltpu.SemaphoreType.DMA((2, CA // 8))]
    return pl.pallas_call(
        functools.partial(step_kernel, False),
        out_shape=(HALF, HALF, frame, edge),
        in_specs=[ANYWHERE] * 5,
        out_specs=[ANYWHERE] * 4,
        scratch_shapes=scratch,
        compiler_params=FULL,
        name="first_step",
    )(state, *coefficients)


def last_step(ts, uv, coefficients, sent, frame, corners, forcing):
    scratch = [pltpu.VMEM((PLANES, CA + 16, CB), jnp.float32), pltpu.VMEM((CA, 128), jnp.float32)]
    scratch += [pltpu.VMEM((PLANES, CA, CB), jnp.float32), pltpu.SemaphoreType.DMA((2,)), pltpu.SemaphoreType.DMA((1, CA // 8))]
    return pl.pallas_call(
        functools.partial(step_kernel, True),
        out_shape=jax.ShapeDtypeStruct((PLANES, CA, CB), jnp.float32),
        in_specs=[ANYWHERE] * 2 + [WHOLE] * 11,
        out_specs=ANYWHERE,
        scratch_shapes=scratch,
        compiler_params=STEP,
        name="last_step",
    )(ts, uv, *coefficients, *sent, frame, corners, forcing)


LISTS = (
    jax.ShapeDtypeStruct((STEPS, VALS, 32, CHUNK), jnp.float32),
    jax.ShapeDtypeStruct((STEPS, VALS, 32, CHUNK), jnp.float32),
    jax.ShapeDtypeStruct((STEPS, 1, 32, CHUNK), jnp.float32),
    jax.ShapeDtypeStruct((8, 128), jnp.int32),
)
WINDOW, UNROLL = 40, 8


def corner_columns(got_ref):
    tx, ty = lax.axis_index("tx"), lax.axis_index("ty")
    rows, columns = lax.axis_size("tx"), lax.axis_size("ty")
    plane = lax.broadcasted_iota(jnp.int32, (PLANES, 128), 0)
    lane = lax.broadcasted_iota(jnp.int32, (PLANES, 128), 1)
    out = jnp.zeros((PLANES, 128), jnp.float32)
    for c, (x, y) in enumerate(((1, 1), (1, -1), (-1, 1), (-1, -1))):
        there = (tx + x >= 0) & (tx + x < rows) & (ty + y >= 0) & (ty + y < columns)
        source = jnp.where(there, (tx + x) * columns + ty + y, 0)
        row = got_ref[pl.ds(source * WIRE + WORDS, 1), :]
        picked = jnp.sum(jnp.where(lane == plane + c * PLANES, row, 0.0), axis=1, keepdims=True)
        out = jnp.where((lane == c) & there, picked, out)
    return out


def order_all_kernel(got_any, high_ref, low_ref, cell_ref, edge_ref, corner_ref, got_ref, sem):
    load = pltpu.make_async_copy(got_any, got_ref, sem)
    load.start()
    load.wait()
    order_kernel(got_ref, high_ref, low_ref, cell_ref)
    bounds_of(cell_ref, edge_ref)
    corner_ref[...] = corner_columns(got_ref)


def order(got):
    *lists, corners = pl.pallas_call(
        order_all_kernel,
        out_shape=LISTS + (jax.ShapeDtypeStruct((PLANES, 128), jnp.float32),),
        in_specs=[ANYWHERE],
        out_specs=[WHOLE] * 5,
        scratch_shapes=[pltpu.VMEM(got.shape, jnp.float32), pltpu.SemaphoreType.DMA(())],
        compiler_params=PARAMS,
        name="order",
    )(got)
    return lists, corners


def first_records_kernel(high_ref, low_ref, cell_ref, edge_ref, still_ref, frame_ref, uv_edge_ref, ts_ref, top_ref, bottom_ref, left_ref, right_ref):
    half = PLANES // 2
    ts_ref[...] = still_ref[...]
    spread_step(0, 0, 32, WINDOW, UNROLL, high_ref, low_ref, cell_ref, edge_ref, ts_ref)

    def plane(p, rows, cols):
        return ts_ref[p, rows, cols]

    row_lines(plane, half, top_ref, bottom_ref)
    left_ref[:half, :], right_ref[:half, :] = column_lines(plane, half)
    for n, (line, side) in enumerate(((top_ref, left_ref), (bottom_ref, right_ref))):
        line[half:PLANES, :] = uv_edge_ref[n * half : (n + 1) * half, :]
        line[PLANES:, :] = frame_ref[n * FRAME : (n + 1) * FRAME, :]
        side[half:PLANES, :] = uv_edge_ref[PLANES:, n * CA : (n + 1) * CA]
        side[PLANES:, :] = frame_ref[2 * FRAME :, n * CA : (n + 1) * CA]


EDGES = (jax.ShapeDtypeStruct((PLANES + FRAME, CB), jnp.float32),) * 2 + (jax.ShapeDtypeStruct((PLANES + FRAME, CA), jnp.float32),) * 2


def first_records(lists, still, frame, uv_edges):
    ts, *edges = pl.pallas_call(
        first_records_kernel,
        out_shape=(HALF,) + EDGES,
        in_specs=[WHOLE] * 3 + [pl.BlockSpec(memory_space=pltpu.SMEM)] + [WHOLE] * 3,
        out_specs=[WHOLE] * 5,
        compiler_params=PARAMS,
        name="first_records",
    )(*lists, still, frame, uv_edges)
    return ts, edges


def second_records_kernel(part, high_ref, low_ref, cell_ref, edge_ref, *rest):
    out_ref = rest[-1]
    out_ref[...] = rest[0][...] if part else jnp.zeros_like(out_ref)
    spread_step(1, 16 * part, 16 * part + 16, WINDOW, UNROLL, high_ref, low_ref, cell_ref, edge_ref, out_ref)


def second_records(lists, part, earlier=()):
    return pl.pallas_call(
        functools.partial(second_records_kernel, part),
        out_shape=jax.ShapeDtypeStruct((PLANES // 2, CA, CB), jnp.float32),
        in_specs=[WHOLE] * 3 + [pl.BlockSpec(memory_space=pltpu.SMEM)] + [WHOLE] * len(earlier),
        out_specs=WHOLE,
        input_output_aliases={4: 0} if earlier else {},
        compiler_params=PARAMS,
        name="second_records",
    )(*lists, *earlier)


def local(adjoint_start, mixing_h, mixing_v, courant, coriolis, misfit, owner, column):
    devices = lax.axis_size("tx") * lax.axis_size("ty")
    state = adjoint_start.reshape(PLANES, CA, CB)
    coefficients = (mixing_h, mixing_v, courant, coriolis)
    sent = pack(owner.transpose(0, 2, 1), column, misfit, state, devices)
    got = lax.all_to_all(sent.reshape(devices, 1, WIRE * 128), ("tx", "ty"), split_axis=0, concat_axis=0, tiled=True)
    still, uv, frame, uv_edges = first_step(state, coefficients)
    lists, corners = order(got.reshape(devices * WIRE, 128))
    ts, (top, bottom, left, right) = first_records(lists, still, frame, uv_edges)
    before, after_ = moved(bottom, "tx", True), moved(top, "tx", False)
    prior = moved(right, "ty", True)
    forcing = second_records(lists, 0)
    left, forcing = after(left, forcing)
    next_ = moved(left, "ty", False)
    forcing = second_records(lists, 1, (forcing,))
    return last_step(ts, uv, coefficients, (before, after_, prior, next_), frame, corners, forcing).reshape(FIELDS, LEV, CA, CB)


def solution(mesh):
    return jax.shard_map(
        local,
        mesh=mesh,
        in_specs=(
            P(None, None, "tx", "ty"),
            P(None, "tx", "ty"),
            P(None, "tx", "ty"),
            P(None, None, "tx", "ty"),
            P("tx", "ty"),
            P(None, None, ("tx", "ty")),
            P(None, ("tx", "ty"), None),
            P(None, ("tx", "ty")),
        ),
        out_specs=P(None, None, "tx", "ty"),
        check_vma=False,
    )
```

```python
import functools
import jax
import jax.numpy as jnp
from jax import lax
from jax.experimental import pallas as pl
from jax.experimental.pallas import tpu as pltpu
from jax.sharding import PartitionSpec as P

CA, CB, LEV, STEPS, CAP = 128, 256, 4, 2, 64
FIELDS = 4
PLANES = FIELDS * LEV
VALS = 2 * LEV
WORDS = VALS + 1
WIRE = WORDS + 1
CHUNK = 256
BF = jnp.bfloat16
NT = (((1,), (1,)), ((), ()))
LIMIT = 24
WHOLE = pl.BlockSpec(memory_space=pltpu.VMEM)
ANYWHERE = pl.BlockSpec(memory_space=pltpu.HBM)
PARAMS = pltpu.CompilerParams(vmem_limit_bytes=LIMIT << 20)
STEP = pltpu.CompilerParams(vmem_limit_bytes=40 << 20)
FULL = pltpu.CompilerParams(vmem_limit_bytes=63400000)


def halves(x):
    top = x.astype(BF)
    return top, (x - top.astype(jnp.float32)).astype(BF)


def slots(owner_ref, place_ref, devices):
    r = lax.broadcasted_iota(jnp.int32, (CHUNK, CHUNK), 0)
    c = lax.broadcasted_iota(jnp.int32, (CHUNK, CHUNK), 1)
    earlier = (r < c).astype(jnp.float32).astype(BF)
    tiles = lax.broadcasted_iota(jnp.int32, (devices, CHUNK), 0)
    counts = [jnp.zeros((devices, 1), jnp.float32)] * STEPS
    for i in range(owner_ref.shape[2] // CHUNK):
        at = pl.ds(i * CHUNK, CHUNK)
        for t in range(STEPS):
            target = owner_ref[t, :, at]
            hot = tiles == target
            ones = hot.astype(jnp.float32)
            before = jnp.dot(ones.astype(BF), earlier, preferred_element_type=jnp.float32)
            slot = jnp.sum(jnp.where(hot, before + counts[t], 0.0), axis=0, keepdims=True)
            counts[t] = counts[t] + before[:, CHUNK - 1 :] + ones[:, CHUNK - 1 :]
            place_ref[t, :, at] = (target & 3) * CAP + slot.astype(jnp.int32)


def gather(span, owner_ref, place_ref, column_ref, misfit_ref, acc_ref):
    groups = acc_ref.shape[1] // WORDS
    group_row = lax.broadcasted_iota(jnp.int32, (groups, span), 0)
    place_row = lax.broadcasted_iota(jnp.int32, (CHUNK, span), 0)

    def part(t, i):
        at = pl.ds(pl.multiple_of(i * span, span), span)
        group_hot = (group_row == (owner_ref[t, :, at] >> 2)).astype(jnp.float32).astype(BF)
        place_hot = (place_row == place_ref[t, :, at]).astype(jnp.float32).astype(BF)
        cell = column_ref[t : t + 1, at]
        high, low = halves(misfit_ref[t, :, at])
        row = (cell - (cell & (CB - 1))).astype(jnp.float32).astype(BF)
        col = ((cell & (CB - 1)) + 1).astype(jnp.float32).astype(BF)
        lhs_h = jnp.concatenate([group_hot * high[k : k + 1] for k in range(VALS)] + [group_hot * row], axis=0)
        lhs_l = jnp.concatenate([group_hot * low[k : k + 1] for k in range(VALS)] + [group_hot * col], axis=0)
        lhs = jnp.concatenate([lhs_h, lhs_l], axis=1)
        rhs = jnp.concatenate([place_hot, place_hot], axis=1)
        return lax.dot_general(lhs, rhs, NT, preferred_element_type=jnp.float32)

    def body(i, carry):
        for t in range(STEPS):
            acc_ref[t] += part(t, i)
        return carry

    for t in range(STEPS):
        acc_ref[t] = part(t, 0)
    lax.fori_loop(1, owner_ref.shape[2] // span, body, 0)


def corner_row(first, final):
    plane = lax.broadcasted_iota(jnp.int32, (PLANES, 128), 0)
    lane = lax.broadcasted_iota(jnp.int32, (PLANES, 128), 1)
    row = jnp.zeros((PLANES, 128), jnp.float32)
    for c, x in enumerate((first[:, :1], first[:, CB - 1 :], final[:, :1], final[:, CB - 1 :])):
        row = jnp.where(lane == plane + c * PLANES, x, row)
    return jnp.sum(row, axis=0, keepdims=True)


def pack_kernel(devices, span, owner_any, column_any, misfit_any, state_any, out_any, owner_ref, column_ref, misfit_ref, place_ref, acc_ref, out_ref, tile_ref, sem):
    pairs = [(owner_any, owner_ref), (column_any, column_ref), (misfit_any, misfit_ref)]
    pairs += [(state_any.at[:, pl.ds(at, 8)], tile_ref.at[n]) for n, at in enumerate((0, CA - 8))]
    loads = [pltpu.make_async_copy(x, y, sem.at[n]) for n, (x, y) in enumerate(pairs)]
    for load in loads:
        load.start()
    loads[0].wait()
    slots(owner_ref, place_ref, devices)
    for load in loads[1:]:
        load.wait()
    first = jnp.concatenate([tile_ref[0, p, :1, :] for p in range(PLANES)], axis=0)
    final = jnp.concatenate([tile_ref[1, p, 7:, :] for p in range(PLANES)], axis=0)
    out_ref[pl.ds(WORDS, devices, stride=WIRE), :] = jnp.broadcast_to(corner_row(first, final), (devices, 128))
    gather(span, owner_ref, place_ref, column_ref, misfit_ref, acc_ref)
    groups = devices // 4
    left = lax.broadcasted_iota(jnp.int32, (groups, 128), 1) < CAP
    for k in range(WORDS):
        for j in range(2):
            a = acc_ref[0, pl.ds(k * groups, groups), pl.ds(j * 128, 128)]
            b = acc_ref[1, pl.ds(k * groups, groups), pl.ds(j * 128, 128)]
            out_ref[pl.ds(2 * j * WIRE + k, groups, stride=4 * WIRE), :] = jnp.where(left, a, pltpu.roll(b, CAP, 1))
            out_ref[pl.ds((2 * j + 1) * WIRE + k, groups, stride=4 * WIRE), :] = jnp.where(left, pltpu.roll(a, CAP, 1), b)
    store = pltpu.make_async_copy(out_ref, out_any, sem.at[5])
    store.start()
    store.wait()


def pack(owner, column, misfit, state, devices, span=1024):
    sent = jax.ShapeDtypeStruct((devices * WIRE, 128), jnp.float32)
    return pl.pallas_call(
        functools.partial(pack_kernel, devices, span),
        out_shape=sent,
        in_specs=[ANYWHERE] * 4,
        out_specs=ANYWHERE,
        scratch_shapes=[
            pltpu.VMEM(owner.shape, jnp.int32),
            pltpu.VMEM(column.shape, jnp.int32),
            pltpu.VMEM(misfit.shape, jnp.float32),
            pltpu.VMEM(owner.shape, jnp.int32),
            pltpu.VMEM((STEPS, WORDS * devices // 4, CHUNK), jnp.float32),
            pltpu.VMEM(sent.shape, jnp.float32),
            pltpu.VMEM((2, PLANES, 8, CB), jnp.float32),
            pltpu.SemaphoreType.DMA((6,)),
        ],
        compiler_params=FULL,
        name="pack",
    )(owner, column, misfit, state)


def exchange(keys, span, reach):
    sub = lax.broadcasted_iota(jnp.int32, (8, 128), 0)
    count = len(keys)
    keys = list(keys)
    if reach < count:
        for v in range(count):
            w = v ^ reach
            if v > w:
                continue
            low, high = jnp.minimum(keys[v], keys[w]), jnp.maximum(keys[v], keys[w])
            if span < count:
                keys[v], keys[w] = (high, low) if v & span else (low, high)
            elif span < 8 * count:
                down = (sub & (span // count)) != 0
                keys[v], keys[w] = jnp.where(down, high, low), jnp.where(down, low, high)
            else:
                keys[v], keys[w] = low, high
        return keys
    step = reach // count
    upper = (sub & step) != 0
    if span < 8 * count:
        upper = upper != ((sub & (span // count)) != 0)
    for v in range(count):
        other = jnp.where((sub & step) != 0, pltpu.roll(keys[v], step, 0), pltpu.roll(keys[v], 8 - step, 0))
        keys[v] = jnp.where(upper, jnp.maximum(keys[v], other), jnp.minimum(keys[v], other))
    return keys


def sort_rows(keys):
    span = 2
    while span <= 8 * len(keys):
        reach = span // 2
        while reach:
            keys = exchange(keys, span, reach)
            reach //= 2
        span *= 2
    return keys


def order_kernel(got_ref, high_ref, low_ref, cell_ref):
    lanes = lax.broadcasted_iota(jnp.int32, (128, 128), 1)
    left = lanes < CAP

    def list_of(k):
        a = got_ref[pl.ds(k, 64, stride=WIRE), :]
        b = got_ref[pl.ds(64 * WIRE + k, 64, stride=WIRE), :]
        first = jnp.where(left[:64], a, pltpu.roll(b, CAP, 1))
        second = jnp.where(left[:64], pltpu.roll(a, CAP, 1), b)
        return jnp.concatenate([first, second], axis=0)

    ids = list_of(VALS).astype(jnp.int32)
    slot = lanes & (CAP - 1)
    spread = ((slot & 1) << 5) | ((slot & 2) << 3) | ((slot & 4) << 1) | ((slot & 8) >> 1) | ((slot & 16) >> 3) | ((slot & 32) >> 5)
    idle = ((spread << 1) | (lanes >> 6)) << 8
    key = (jnp.where(ids > 0, ids - 1, idle) << 7) | lanes
    turned = key.astype(jnp.float32).T
    keys = sort_rows([turned[8 * v : 8 * v + 8] for v in range(16)])
    keys = jnp.concatenate(keys, axis=0).astype(jnp.int32)
    source = (keys & 127).astype(jnp.float32).T.astype(jnp.int32)

    def place(ref, k, x):
        for v in range(0, 16, 2):
            a, b = x[8 * v : 8 * v + 8], x[8 * v + 8 : 8 * v + 16]
            g, h = v // 4, (v // 2) % 2
            l8 = left[:8]
            ref[0, k, pl.ds(8 * g, 8), pl.ds(128 * h, 128)] = jnp.where(l8, a, pltpu.roll(b, CAP, 1))
            ref[1, k, pl.ds(8 * g, 8), pl.ds(128 * h, 128)] = jnp.where(l8, pltpu.roll(a, CAP, 1), b)

    place(cell_ref, 0, (keys >> 7).astype(jnp.float32))
    for k in range(VALS):
        moved = jnp.take_along_axis(list_of(k), source, axis=1).T
        top = moved.astype(BF).astype(jnp.float32)
        place(high_ref, k, top)
        place(low_ref, k, moved - top)


def bounds_of(cell_ref, edge_ref):
    chunk = lax.broadcasted_iota(jnp.int32, (32, 128), 0)
    lane = lax.broadcasted_iota(jnp.int32, (32, 128), 1)
    lines = []
    for t in range(STEPS):
        row = cell_ref[t, 0].astype(jnp.int32) >> 8
        least = jnp.min(jnp.minimum(row[:, :128], row[:, 128:]).astype(jnp.float32), axis=1, keepdims=True)
        most = jnp.max(jnp.maximum(row[:, :128], row[:, 128:]).astype(jnp.float32), axis=1, keepdims=True)
        lines += [jnp.sum(jnp.where(chunk == lane, e, 0.0), axis=0, keepdims=True) for e in (least, most)]
    edge_ref[...] = jnp.concatenate(lines + [jnp.zeros((4, 128), jnp.float32)], axis=0).astype(jnp.int32)


def products(t, i, base, window, keep, high_ref, low_ref, cell_ref):
    row_iota = lax.broadcasted_iota(jnp.int32, (window, CHUNK), 0) + base
    col_iota = lax.broadcasted_iota(jnp.int32, (CB, CHUNK), 0)
    cell = cell_ref[t, 0, pl.ds(i, 1), :].astype(jnp.int32)
    col_hot = (col_iota == (cell & (CB - 1))).astype(jnp.float32).astype(BF)
    hit = row_iota == (cell >> 8)
    if keep is not None:
        hit = hit & (row_iota >= keep)
    row_hot = hit.astype(jnp.float32).astype(BF)
    lhs = jnp.concatenate([row_hot * ref[t, k, pl.ds(i, 1), :].astype(BF) for ref in (high_ref, low_ref) for k in range(VALS)], axis=0)
    out = lax.dot_general(lhs, col_hot, NT, preferred_element_type=jnp.float32)
    return out[: VALS * window] + out[VALS * window :]


def spread_step(t, chunks_from, chunks_to, window, unroll, high_ref, low_ref, cell_ref, edge_ref, acc_ref):
    def gain(base, out):
        for k in range(VALS):
            acc_ref[k, pl.ds(base, window), :] += out[k * window : (k + 1) * window]

    def first(i):
        return pl.multiple_of(jnp.minimum((edge_ref[2 * t, i] >> 3) << 3, CA - window), 8)

    def body(j, carry):
        chunks = [j * unroll + u for u in range(unroll)]
        bases = [first(i) for i in chunks]
        outs = [products(t, i, base, window, None, high_ref, low_ref, cell_ref) for i, base in zip(chunks, bases)]
        for base, out in zip(bases, outs):
            gain(base, out)
        return carry

    lax.fori_loop(chunks_from // unroll, chunks_to // unroll, body, 0)

    def rest(i, carry):
        def more(start):
            base = pl.multiple_of(jnp.minimum(start, CA - window), 8)
            gain(base, products(t, i, base, window, start, high_ref, low_ref, cell_ref))
            return start + window

        lax.while_loop(lambda start: start <= edge_ref[2 * t + 1, i], more, first(i) + window)
        return carry

    lax.fori_loop(chunks_from, chunks_to, rest, 0)


def row_lines(plane, count, top_ref, bottom_ref):
    for p in range(count):
        top_ref[p : p + 1, :] = plane(p, pl.ds(0, 8), pl.ds(0, CB))[:1]
        bottom_ref[p : p + 1, :] = plane(p, pl.ds(CA - 8, 8), pl.ds(0, CB))[7:]


def column_lines(plane, count):
    lane = lax.broadcasted_iota(jnp.int32, (CA, 128), 1)
    picked = jnp.zeros((CA, 128), jnp.float32)
    for p in range(count):
        picked = jnp.where(lane == p, plane(p, pl.ds(0, CA), pl.ds(0, 128))[:, :1], picked)
        picked = jnp.where(lane == count + p, plane(p, pl.ds(0, CA), pl.ds(CB - 128, 128))[:, 127:], picked)
    lines = picked.T
    return lines[:count], lines[count : 2 * count]


def swapped(x, axis, odd):
    count = lax.axis_size(axis)
    pairs = [(i, (i + 1) % count) for i in range(odd, count, 2)]
    return lax.ppermute(x, axis, pairs + [(j, i) for i, j in pairs])


def after(x, *others):
    return lax.optimization_barrier((x, *others))


FRAME = PLANES + 2 * LEV


def per_plane(levels):
    return jnp.concatenate([levels] * FIELDS, axis=0)


def write_frame(plane, mix_h_ref, courant_ref, frame_ref):
    columns = column_lines(plane, PLANES)
    mix = column_lines(lambda k, rows, cols: mix_h_ref[k, rows, cols], LEV)
    along = column_lines(lambda k, rows, cols: courant_ref[0, k, rows, cols], LEV)
    across = column_lines(lambda k, rows, cols: courant_ref[1, k, rows, cols], LEV)
    place = lax.broadcasted_iota(jnp.int32, (LEV, CA), 1)
    for n, sign in ((0, -0.5), (1, 0.5)):
        ends = jnp.where(place == 0, mix[n] - 0.5 * along[n], jnp.where(place == CA - 1, mix[n] + 0.5 * along[n], 0.0))
        frame_ref[2 * FRAME : 3 * FRAME, n * CA : (n + 1) * CA] = jnp.concatenate([columns[n], mix[n] + sign * across[n], ends], axis=0)
    place = lax.broadcasted_iota(jnp.int32, (LEV, CB), 1)
    for n, sign, at in ((0, -0.5, 0), (1, 0.5, 7)):
        rows = pl.ds((CA - 8) * n, 8)

        def line(read, count):
            return jnp.concatenate([read(k, rows, pl.ds(0, CB))[at : at + 1] for k in range(count)], axis=0)

        mix = line(lambda k, rows, cols: mix_h_ref[k, rows, cols], LEV)
        along = line(lambda k, rows, cols: courant_ref[0, k, rows, cols], LEV)
        across = line(lambda k, rows, cols: courant_ref[1, k, rows, cols], LEV)
        ends = jnp.where(place == 0, mix - 0.5 * across, jnp.where(place == CB - 1, mix + 0.5 * across, 0.0))
        frame_ref[n * FRAME : (n + 1) * FRAME, :] = jnp.concatenate([line(plane, PLANES), mix + sign * along, ends], axis=0)


def ends_of(length, first, final):
    place = lax.broadcasted_iota(jnp.int32, (PLANES, length), 1)
    return jnp.where(place == 0, first, jnp.where(place == length - 1, final, 0.0))


def beside(sent, own, corners):
    edge, factor, ends = sent[:PLANES], sent[2 * PLANES : 2 * PLANES + LEV], sent[2 * PLANES + LEV :]
    return edge + per_plane(factor) * own[:PLANES] + per_plane(ends) * corners


def gained(sent, own):
    return per_plane(own[PLANES : PLANES + LEV]) * sent[PLANES : 2 * PLANES]


def step_kernel(last, *refs):
    half = PLANES // 2
    if last:
        ts_any, uv_any, mix_h_ref, mix_v_ref, courant_ref, turn_ref, *sent_refs, frame_ref, corner_ref, forcing_ref, out_any, state_ref, column_ref, out_ref, sem, out_sem = refs
        uv_any_half = uv_any
    else:
        ts_any, mix_h_any, mix_v_any, courant_any, turn_any, ts_out, uv_out, frame_any = refs[:8]
        state_ref, mix_h_ref, mix_v_ref, courant_ref, turn_ref, frame_ref, out_ref, sem, out_sem = refs[8:]
        uv_any_half = ts_any.at[pl.ds(half, half)]
    pairs = [(ts_any.at[pl.ds(0, half)], state_ref.at[pl.ds(0, half), pl.ds(8, CA)]), (uv_any_half, state_ref.at[pl.ds(half, half), pl.ds(8, CA)])]
    if not last:
        pairs += [(mix_h_any, mix_h_ref), (mix_v_any, mix_v_ref), (courant_any, courant_ref), (turn_any, turn_ref)]
    loads = [pltpu.make_async_copy(x, y, sem.at[n]) for n, (x, y) in enumerate(pairs)]
    for load in loads:
        load.start()
    if last:
        tx, ty = lax.axis_index("tx"), lax.axis_index("ty")
        there = tx > 0, tx < lax.axis_size("tx") - 1, ty > 0, ty < lax.axis_size("ty") - 1
        sent = []
        for place, even_ref, odd_ref in ((tx, *sent_refs[:2]), (ty, *sent_refs[2:])):
            even, odd = even_ref[...], odd_ref[...]
            is_odd = lax.rem(place, 2) == 1
            sent += [jnp.where(is_odd, even, odd), jnp.where(is_odd, odd, even)]
        before, after, prior, next_ = [jnp.where(flag, x, 0.0) for x, flag in zip(sent, there)]
        top, bottom = frame_ref[:FRAME], frame_ref[FRAME : 2 * FRAME]
        left, right = frame_ref[2 * FRAME : 3 * FRAME, :CA], frame_ref[2 * FRAME : 3 * FRAME, CA:]
        corner = [corner_ref[:, c : c + 1] for c in range(4)]
        beside_prior = beside(prior, left, ends_of(CA, corner[3], corner[1]))
        beside_next = beside(next_, right, ends_of(CA, corner[2], corner[0]))
        spare = jnp.zeros((128 - 4 * PLANES, CA), jnp.float32)
        column_ref[...] = jnp.concatenate([beside_prior, beside_next, gained(prior, left), gained(next_, right), spare], axis=0).T
        beside_before = beside(before, top, ends_of(CB, corner[3], corner[2]))
        beside_after = beside(after, bottom, ends_of(CB, corner[1], corner[0]))
        gain_before, gain_after = gained(before, top), gained(after, bottom)
        for p in range(PLANES):
            state_ref[p, 0:8, :] = jnp.broadcast_to(beside_before[p : p + 1, :], (8, CB))
            state_ref[p, CA + 8 : CA + 16, :] = jnp.broadcast_to(beside_after[p : p + 1, :], (8, CB))
    else:
        state_ref[:, 0:8, :] = jnp.zeros((PLANES, 8, CB), jnp.float32)
        state_ref[:, CA + 8 : CA + 16, :] = jnp.zeros((PLANES, 8, CB), jnp.float32)
    for load in loads:
        load.wait()
    if last:
        edge = lax.broadcasted_iota(jnp.int32, (CA, 128), 1)
        for p in range(PLANES):
            for lanes, at, n in ((pl.ds(0, 128), 0, 2), (pl.ds(CB - 128, 128), 127, 3)):
                gain = column_ref[:, n * PLANES + p : n * PLANES + p + 1]
                state_ref[p, pl.ds(8, CA), lanes] += jnp.where(edge == at, gain, 0.0)
            state_ref[p, 8:9, :] += gain_before[p : p + 1, :]
            state_ref[p, CA + 7 : CA + 8, :] += gain_after[p : p + 1, :]
    else:
        write_frame(lambda p, rows, cols: state_ref[p, pl.ds(8 + rows.start, rows.size), cols], mix_h_ref, courant_ref, frame_ref)
    sub = lax.broadcasted_iota(jnp.int32, (8, CB), 0)
    lane = lax.broadcasted_iota(jnp.int32, (8, CB), 1)

    def store_of(i):
        rows = pl.ds(pl.multiple_of(i * 8, 8), 8)
        if last:
            return [pltpu.make_async_copy(out_ref.at[:, rows], out_any.at[:, rows], out_sem.at[0, i])]
        parts = (pl.ds(0, half), ts_out), (pl.ds(half, half), uv_out)
        return [pltpu.make_async_copy(out_ref.at[planes, rows], out.at[:, rows], out_sem.at[n, i]) for n, (planes, out) in enumerate(parts)]

    def strip(i, carry):
        at = pl.multiple_of(i * 8, 8)
        rows = pl.ds(at, 8)
        sides = column_ref[rows, :] if last else None
        turn = turn_ref[rows, :]
        mix_v = [mix_v_ref[k, rows, :] for k in range(LEV - 1)]
        centre = [state_ref[p, pl.ds(at + 8, 8), :] for p in range(PLANES)]
        for k in range(LEV):
            mix_h = mix_h_ref[k, rows, :]
            c0 = 0.5 * courant_ref[0, k, rows, :]
            c1 = 0.5 * courant_ref[1, k, rows, :]
            for f in range(FIELDS):
                p = f * LEV + k
                a = centre[p]
                below = state_ref[p, rows, :]
                above = state_ref[p, pl.ds(at + 16, 8), :]
                up = jnp.where(sub == 7, pltpu.roll(above, 7, 0), pltpu.roll(a, 7, 0))
                down = jnp.where(sub == 0, pltpu.roll(below, 1, 0), pltpu.roll(a, 1, 0))
                right = jnp.where(lane == CB - 1, sides[:, PLANES + p : PLANES + p + 1] if last else 0.0, pltpu.roll(a, CB - 1, 1))
                left = jnp.where(lane == 0, sides[:, p : p + 1] if last else 0.0, pltpu.roll(a, 1, 1))
                new = a + mix_h * (up + down + right + left - 4.0 * a) + c0 * (up - down) + c1 * (right - left)
                if k < LEV - 1:
                    new = new + mix_v[k] * (centre[p + 1] - a)
                if k > 0:
                    new = new - mix_v[k - 1] * (a - centre[p - 1])
                if f == 2:
                    new = new + turn * centre[p + LEV]
                if f == 3:
                    new = new - turn * centre[p - LEV]
                if last and f < 2:
                    new = new + forcing_ref[p, rows, :]
                out_ref[p, rows, :] = new
        for store in store_of(i):
            store.start()
        return carry

    def finish(i, carry):
        for store in store_of(i):
            store.wait()
        return carry

    lax.fori_loop(0, CA // 8, strip, 0, unroll=2)
    if not last:

        def plane(p, rows, cols):
            return out_ref[half + p, rows, cols]

        at = 3 * FRAME
        row_lines(plane, half, frame_ref.at[pl.ds(at, half)], frame_ref.at[pl.ds(at + half, half)])
        frame_ref[at + PLANES :, :CA], frame_ref[at + PLANES :, CA:] = column_lines(plane, half)
        frame_store = pltpu.make_async_copy(frame_ref, frame_any, sem.at[6])
        frame_store.start()
    lax.fori_loop(0, CA // 8, finish, 0)
    if not last:
        frame_store.wait()


HALF = jax.ShapeDtypeStruct((PLANES // 2, CA, CB), jnp.float32)


def first_step(state, coefficients):
    frame = jax.ShapeDtypeStruct((3 * FRAME + PLANES + PLANES // 2, CB), jnp.float32)
    scratch = [pltpu.VMEM((PLANES, CA + 16, CB), jnp.float32)] + [pltpu.VMEM(x.shape, jnp.float32) for x in (*coefficients, frame)]
    scratch += [pltpu.VMEM((PLANES, CA, CB), jnp.float32), pltpu.SemaphoreType.DMA((8,)), pltpu.SemaphoreType.DMA((2, CA // 8))]
    return pl.pallas_call(
        functools.partial(step_kernel, False),
        out_shape=(HALF, HALF, frame),
        in_specs=[ANYWHERE] * 5,
        out_specs=[ANYWHERE] * 3,
        scratch_shapes=scratch,
        compiler_params=FULL,
        name="first_step",
    )(state, *coefficients)


def last_step(ts, uv, coefficients, sent, frame, corners, forcing):
    scratch = [pltpu.VMEM((PLANES, CA + 16, CB), jnp.float32), pltpu.VMEM((CA, 128), jnp.float32)]
    scratch += [pltpu.VMEM((PLANES, CA, CB), jnp.float32), pltpu.SemaphoreType.DMA((2,)), pltpu.SemaphoreType.DMA((1, CA // 8))]
    return pl.pallas_call(
        functools.partial(step_kernel, True),
        out_shape=jax.ShapeDtypeStruct((PLANES, CA, CB), jnp.float32),
        in_specs=[ANYWHERE] * 2 + [WHOLE] * 11,
        out_specs=ANYWHERE,
        scratch_shapes=scratch,
        compiler_params=STEP,
        name="last_step",
    )(ts, uv, *coefficients, *sent, frame, corners, forcing)


LISTS = (
    jax.ShapeDtypeStruct((STEPS, VALS, 32, CHUNK), jnp.float32),
    jax.ShapeDtypeStruct((STEPS, VALS, 32, CHUNK), jnp.float32),
    jax.ShapeDtypeStruct((STEPS, 1, 32, CHUNK), jnp.float32),
    jax.ShapeDtypeStruct((8, 128), jnp.int32),
)
WINDOW, UNROLL = 40, 8


def corner_columns(got_ref):
    tx, ty = lax.axis_index("tx"), lax.axis_index("ty")
    rows, columns = lax.axis_size("tx"), lax.axis_size("ty")
    plane = lax.broadcasted_iota(jnp.int32, (PLANES, 128), 0)
    lane = lax.broadcasted_iota(jnp.int32, (PLANES, 128), 1)
    out = jnp.zeros((PLANES, 128), jnp.float32)
    for c, (x, y) in enumerate(((1, 1), (1, -1), (-1, 1), (-1, -1))):
        there = (tx + x >= 0) & (tx + x < rows) & (ty + y >= 0) & (ty + y < columns)
        source = jnp.where(there, (tx + x) * columns + ty + y, 0)
        row = got_ref[pl.ds(source * WIRE + WORDS, 1), :]
        picked = jnp.sum(jnp.where(lane == plane + c * PLANES, row, 0.0), axis=1, keepdims=True)
        out = jnp.where((lane == c) & there, picked, out)
    return out


def first_records_kernel(got_any, still_any, frame_any, ts_ref, high_ref, low_ref, cell_ref, edge_ref, corner_ref, top_ref, bottom_ref, left_ref, right_ref, got_ref, frame_ref, smem_ref, sem):
    pairs = (got_any, got_ref), (still_any, ts_ref), (frame_any, frame_ref)
    loads = [pltpu.make_async_copy(x, y, sem.at[n]) for n, (x, y) in enumerate(pairs)]
    for load in loads:
        load.start()
    loads[0].wait()
    order_kernel(got_ref, high_ref, low_ref, cell_ref)
    bounds_of(cell_ref, edge_ref)
    copy = pltpu.make_async_copy(edge_ref, smem_ref, sem.at[3])
    copy.start()
    corner_ref[...] = corner_columns(got_ref)
    for load in loads[1:]:
        load.wait()
    copy.wait()
    half = PLANES // 2
    spread_step(0, 0, 32, WINDOW, UNROLL, high_ref, low_ref, cell_ref, smem_ref, ts_ref)

    def plane(p, rows, cols):
        return ts_ref[p, rows, cols]

    at = 3 * FRAME
    lines, sides = [], []
    columns = column_lines(plane, half)
    for n in range(2):
        rows = pl.ds((CA - 8) * n, 8)
        edge = [plane(p, rows, pl.ds(0, CB))[7 * n : 7 * n + 1] for p in range(half)]
        lines.append(jnp.concatenate(edge + [frame_ref[at + n * half : at + (n + 1) * half, :], frame_ref[n * FRAME : (n + 1) * FRAME, :]], axis=0))
        lanes = slice(n * CA, (n + 1) * CA)
        sides.append(jnp.concatenate([columns[n], frame_ref[at + PLANES :, lanes], frame_ref[2 * FRAME : 3 * FRAME, lanes]], axis=0))
    for axis, (first, final), even_ref, odd_ref in (("tx", lines, top_ref, bottom_ref), ("ty", sides, left_ref, right_ref)):
        odd = lax.rem(lax.axis_index(axis), 2) == 1
        even_ref[...] = jnp.where(odd, first, final)
        odd_ref[...] = jnp.where(odd, final, first)


EDGES = (jax.ShapeDtypeStruct((PLANES + FRAME, CB), jnp.float32),) * 2 + (jax.ShapeDtypeStruct((PLANES + FRAME, CA), jnp.float32),) * 2


def first_records(got, still, frame):
    out = pl.pallas_call(
        first_records_kernel,
        out_shape=(HALF,) + LISTS + (jax.ShapeDtypeStruct((PLANES, 128), jnp.float32),) + EDGES,
        in_specs=[ANYWHERE] * 3,
        out_specs=[WHOLE] * 10,
        scratch_shapes=[
            pltpu.VMEM(got.shape, jnp.float32),
            pltpu.VMEM(frame.shape, jnp.float32),
            pltpu.SMEM((8, 128), jnp.int32),
            pltpu.SemaphoreType.DMA((4,)),
        ],
        compiler_params=PARAMS,
        name="first_records",
    )(got, still, frame)
    return out[0], out[1:5], out[5], out[6:]


def second_records_kernel(high_ref, low_ref, cell_ref, edge_ref, out_ref):
    out_ref[...] = jnp.zeros_like(out_ref)
    spread_step(1, 0, 32, WINDOW, UNROLL, high_ref, low_ref, cell_ref, edge_ref, out_ref)


def second_records(lists):
    return pl.pallas_call(
        second_records_kernel,
        out_shape=HALF,
        in_specs=[WHOLE] * 3 + [pl.BlockSpec(memory_space=pltpu.SMEM)],
        out_specs=WHOLE,
        compiler_params=PARAMS,
        name="second_records",
    )(*lists)


def local(adjoint_start, mixing_h, mixing_v, courant, coriolis, misfit, owner, column):
    devices = lax.axis_size("tx") * lax.axis_size("ty")
    state = adjoint_start.reshape(PLANES, CA, CB)
    coefficients = (mixing_h, mixing_v, courant, coriolis)
    sent = pack(owner.transpose(0, 2, 1), column, misfit, state, devices)
    got = lax.all_to_all(sent.reshape(devices, 1, WIRE * 128), ("tx", "ty"), split_axis=0, concat_axis=0, tiled=True)
    still, uv, frame = first_step(state, coefficients)
    ts, lists, corners, edges = first_records(got.reshape(devices * WIRE, 128), still, frame)
    x0 = swapped(edges[0], "tx", 0)
    x1 = swapped(edges[1], "tx", 1)
    y0 = swapped(edges[2], "ty", 0)
    y1 = swapped(edges[3], "ty", 1)
    forcing = second_records(lists)
    return last_step(ts, uv, coefficients, (x0, x1, y0, y1), frame, corners, forcing).reshape(FIELDS, LEV, CA, CB)


def solution(mesh):
    return jax.shard_map(
        local,
        mesh=mesh,
        in_specs=(
            P(None, None, "tx", "ty"),
            P(None, "tx", "ty"),
            P(None, "tx", "ty"),
            P(None, None, "tx", "ty"),
            P("tx", "ty"),
            P(None, None, ("tx", "ty")),
            P(None, ("tx", "ty"), None),
            P(None, ("tx", "ty")),
        ),
        out_specs=P(None, None, "tx", "ty"),
        check_vma=False,
    )
```

```python
import functools
import jax
import jax.numpy as jnp
from jax import lax
from jax.experimental import pallas as pl
from jax.experimental.pallas import tpu as pltpu
from jax.sharding import PartitionSpec as P

CA, CB, LEV, STEPS, CAP = 128, 256, 4, 2, 64
FIELDS = 4
PLANES = FIELDS * LEV
VALS = 2 * LEV
WORDS = VALS + 1
WIRE = WORDS + 1
CHUNK = 256
BF = jnp.bfloat16
NT = (((1,), (1,)), ((), ()))
LIMIT = 24
WHOLE = pl.BlockSpec(memory_space=pltpu.VMEM)
ANYWHERE = pl.BlockSpec(memory_space=pltpu.HBM)
PARAMS = pltpu.CompilerParams(vmem_limit_bytes=LIMIT << 20)
STEP = pltpu.CompilerParams(vmem_limit_bytes=40 << 20)
FULL = pltpu.CompilerParams(vmem_limit_bytes=63400000)


def halves(x):
    top = x.astype(BF)
    return top, (x - top.astype(jnp.float32)).astype(BF)


def slots(owner_ref, place_ref, devices):
    r = lax.broadcasted_iota(jnp.int32, (CHUNK, CHUNK), 0)
    c = lax.broadcasted_iota(jnp.int32, (CHUNK, CHUNK), 1)
    earlier = (r < c).astype(jnp.float32).astype(BF)
    tiles = lax.broadcasted_iota(jnp.int32, (devices, CHUNK), 0)
    counts = [jnp.zeros((devices, 1), jnp.float32)] * STEPS
    for i in range(owner_ref.shape[2] // CHUNK):
        at = pl.ds(i * CHUNK, CHUNK)
        for t in range(STEPS):
            target = owner_ref[t, :, at]
            hot = tiles == target
            ones = hot.astype(jnp.float32)
            before = jnp.dot(ones.astype(BF), earlier, preferred_element_type=jnp.float32)
            slot = jnp.sum(jnp.where(hot, before + counts[t], 0.0), axis=0, keepdims=True)
            counts[t] = counts[t] + before[:, CHUNK - 1 :] + ones[:, CHUNK - 1 :]
            place_ref[t, :, at] = (target & 3) * CAP + slot.astype(jnp.int32)


def gather(span, owner_ref, place_ref, column_ref, misfit_ref, acc_ref):
    groups = acc_ref.shape[1] // WORDS
    group_row = lax.broadcasted_iota(jnp.int32, (groups, span), 0)
    place_row = lax.broadcasted_iota(jnp.int32, (CHUNK, span), 0)

    def part(t, i):
        at = pl.ds(pl.multiple_of(i * span, span), span)
        group_hot = (group_row == (owner_ref[t, :, at] >> 2)).astype(jnp.float32).astype(BF)
        place_hot = (place_row == place_ref[t, :, at]).astype(jnp.float32).astype(BF)
        cell = column_ref[t : t + 1, at]
        high, low = halves(misfit_ref[t, :, at])
        row = (cell - (cell & (CB - 1))).astype(jnp.float32).astype(BF)
        col = ((cell & (CB - 1)) + 1).astype(jnp.float32).astype(BF)
        lhs_h = jnp.concatenate([group_hot * high[k : k + 1] for k in range(VALS)] + [group_hot * row], axis=0)
        lhs_l = jnp.concatenate([group_hot * low[k : k + 1] for k in range(VALS)] + [group_hot * col], axis=0)
        lhs = jnp.concatenate([lhs_h, lhs_l], axis=1)
        rhs = jnp.concatenate([place_hot, place_hot], axis=1)
        return lax.dot_general(lhs, rhs, NT, preferred_element_type=jnp.float32)

    def body(i, carry):
        for t in range(STEPS):
            acc_ref[t] += part(t, i)
        return carry

    for t in range(STEPS):
        acc_ref[t] = part(t, 0)
    lax.fori_loop(1, owner_ref.shape[2] // span, body, 0)


def corner_row(first, final):
    plane = lax.broadcasted_iota(jnp.int32, (PLANES, 128), 0)
    lane = lax.broadcasted_iota(jnp.int32, (PLANES, 128), 1)
    row = jnp.zeros((PLANES, 128), jnp.float32)
    for c, x in enumerate((first[:, :1], first[:, CB - 1 :], final[:, :1], final[:, CB - 1 :])):
        row = jnp.where(lane == plane + c * PLANES, x, row)
    return jnp.sum(row, axis=0, keepdims=True)


def pack_kernel(devices, span, owner_any, column_any, misfit_any, state_any, out_any, owner_ref, column_ref, misfit_ref, place_ref, acc_ref, out_ref, tile_ref, sem):
    pairs = [(owner_any, owner_ref), (column_any, column_ref), (misfit_any, misfit_ref)]
    pairs += [(state_any.at[:, pl.ds(at, 8)], tile_ref.at[n]) for n, at in enumerate((0, CA - 8))]
    loads = [pltpu.make_async_copy(x, y, sem.at[n]) for n, (x, y) in enumerate(pairs)]
    for load in loads:
        load.start()
    loads[0].wait()
    slots(owner_ref, place_ref, devices)
    for load in loads[1:]:
        load.wait()
    first = jnp.concatenate([tile_ref[0, p, :1, :] for p in range(PLANES)], axis=0)
    final = jnp.concatenate([tile_ref[1, p, 7:, :] for p in range(PLANES)], axis=0)
    out_ref[pl.ds(WORDS, devices, stride=WIRE), :] = jnp.broadcast_to(corner_row(first, final), (devices, 128))
    gather(span, owner_ref, place_ref, column_ref, misfit_ref, acc_ref)
    groups = devices // 4
    left = lax.broadcasted_iota(jnp.int32, (groups, 128), 1) < CAP
    for k in range(WORDS):
        for j in range(2):
            a = acc_ref[0, pl.ds(k * groups, groups), pl.ds(j * 128, 128)]
            b = acc_ref[1, pl.ds(k * groups, groups), pl.ds(j * 128, 128)]
            out_ref[pl.ds(2 * j * WIRE + k, groups, stride=4 * WIRE), :] = jnp.where(left, a, pltpu.roll(b, CAP, 1))
            out_ref[pl.ds((2 * j + 1) * WIRE + k, groups, stride=4 * WIRE), :] = jnp.where(left, pltpu.roll(a, CAP, 1), b)
    store = pltpu.make_async_copy(out_ref, out_any, sem.at[5])
    store.start()
    store.wait()


def pack(owner, column, misfit, state, devices, span=2048):
    sent = jax.ShapeDtypeStruct((devices * WIRE, 128), jnp.float32)
    return pl.pallas_call(
        functools.partial(pack_kernel, devices, span),
        out_shape=sent,
        in_specs=[ANYWHERE] * 4,
        out_specs=ANYWHERE,
        scratch_shapes=[
            pltpu.VMEM(owner.shape, jnp.int32),
            pltpu.VMEM(column.shape, jnp.int32),
            pltpu.VMEM(misfit.shape, jnp.float32),
            pltpu.VMEM(owner.shape, jnp.int32),
            pltpu.VMEM((STEPS, WORDS * devices // 4, CHUNK), jnp.float32),
            pltpu.VMEM(sent.shape, jnp.float32),
            pltpu.VMEM((2, PLANES, 8, CB), jnp.float32),
            pltpu.SemaphoreType.DMA((6,)),
        ],
        compiler_params=FULL,
        name="pack",
    )(owner, column, misfit, state)


def exchange(keys, span, reach, flip=None):
    sub = lax.broadcasted_iota(jnp.int32, (8, 128), 0)
    count = len(keys)
    keys = list(keys)
    if span < 8 * count:
        flip = (sub & (span // count)) != 0 if span >= count else None
    if reach < count:
        for v in range(count):
            w = v ^ reach
            if v > w:
                continue
            low, high = jnp.minimum(keys[v], keys[w]), jnp.maximum(keys[v], keys[w])
            if flip is not None:
                low, high = jnp.where(flip, high, low), jnp.where(flip, low, high)
            elif span < count and v & span:
                low, high = high, low
            keys[v], keys[w] = low, high
        return keys
    step = reach // count
    second = (sub & step) != 0
    upper = second if flip is None else second != flip
    for v in range(count):
        other = jnp.where(second, pltpu.roll(keys[v], step, 0), pltpu.roll(keys[v], 8 - step, 0))
        keys[v] = jnp.where(upper, jnp.maximum(keys[v], other), jnp.minimum(keys[v], other))
    return keys


def sort_rows(keys):
    length = 8 * len(keys)
    beyond = (lax.broadcasted_iota(jnp.int32, (8, 128), 1) & 32) != 0
    span = 2
    while span <= length:
        reach = span // 2
        while reach:
            keys = exchange(keys, span, reach, beyond)
            reach //= 2
        span *= 2
    other = [jnp.where(beyond, pltpu.roll(x, 32, 1), pltpu.roll(x, 96, 1)) for x in keys]
    keys = [jnp.where(beyond, jnp.maximum(x, y), jnp.minimum(x, y)) for x, y in zip(keys, other)]
    reach = length // 2
    while reach:
        keys = exchange(keys, length, reach)
        reach //= 2
    return keys


def order_kernel(got_ref, high_ref, low_ref, cell_ref):
    lanes = lax.broadcasted_iota(jnp.int32, (128, 128), 1)
    rows = lax.broadcasted_iota(jnp.int32, (128, 128), 0)
    left = lanes < CAP

    def list_of(k):
        a = got_ref[pl.ds(k, 64, stride=WIRE), :]
        b = got_ref[pl.ds(64 * WIRE + k, 64, stride=WIRE), :]
        first = jnp.where(left[:64], a, pltpu.roll(b, CAP, 1))
        second = jnp.where(left[:64], pltpu.roll(a, CAP, 1), b)
        return jnp.concatenate([first, second], axis=0)

    ids = list_of(VALS).astype(jnp.int32)
    slot = lanes & (CAP - 1)
    spread = ((slot & 1) << 5) | ((slot & 2) << 3) | ((slot & 4) << 1) | ((slot & 8) >> 1) | ((slot & 16) >> 3) | ((slot & 32) >> 5)
    idle = ((spread << 1) | (lanes >> 6)) << 8
    key = (jnp.where(ids > 0, ids - 1, idle) << 8) | ((rows & 32) << 2) | lanes
    turned = key.astype(jnp.float32).T
    keys = sort_rows([turned[8 * v : 8 * v + 8] for v in range(16)])
    keys = jnp.concatenate(keys, axis=0).astype(jnp.int32)
    source = (keys & 255).astype(jnp.float32).T.astype(jnp.int32)
    lane_of, beyond = source & 127, source >= 128
    block = lanes[:8] >> 5

    def place(x, store):
        for h in range(2):
            for u in range(2):
                parts = [x[8 * v : 8 * v + 8] for v in range(8 * h + 4 * u, 8 * h + 4 * u + 4)]
                for group in range(4):
                    moved = [part if j == group else pltpu.roll(part, (j - group) % 4 * 32, 1) for j, part in enumerate(parts)]
                    tile = jnp.where(block < 2, jnp.where(block == 0, moved[0], moved[1]), jnp.where(block == 2, moved[2], moved[3]))
                    store(group // 2, pl.ds(16 * (group % 2) + 8 * h, 8), pl.ds(128 * u, 128), tile)

    def store_cell(t, at, cols, tile):
        cell_ref[t, 0, at, cols] = tile

    place((keys >> 8).astype(jnp.float32), store_cell)
    for k in range(VALS):
        x = list_of(k)
        near = jnp.concatenate([x[:32], x[:32], x[64:96], x[64:96]], axis=0)
        far = jnp.concatenate([x[32:64], x[32:64], x[96:], x[96:]], axis=0)
        picked = jnp.where(beyond, jnp.take_along_axis(far, lane_of, axis=1), jnp.take_along_axis(near, lane_of, axis=1))

        def store_value(t, at, cols, tile, k=k):
            top = tile.astype(BF).astype(jnp.float32)
            high_ref[t, k, at, cols] = top
            low_ref[t, k, at, cols] = tile - top

        place(picked.T, store_value)


def bounds_of(cell_ref, edge_ref):
    chunk = lax.broadcasted_iota(jnp.int32, (32, 128), 0)
    lane = lax.broadcasted_iota(jnp.int32, (32, 128), 1)
    lines, beyond = [], []
    for t in range(STEPS):
        row = cell_ref[t, 0].astype(jnp.int32) >> 8
        least = jnp.min(jnp.minimum(row[:, :128], row[:, 128:]).astype(jnp.float32), axis=1, keepdims=True)
        most = jnp.max(jnp.maximum(row[:, :128], row[:, 128:]).astype(jnp.float32), axis=1, keepdims=True)
        lines += [jnp.sum(jnp.where(chunk == lane, e, 0.0), axis=0, keepdims=True) for e in (least, most)]
        base = jnp.minimum((least.astype(jnp.int32) >> 3) << 3, CA - WINDOW)
        over = jnp.max((most.astype(jnp.int32) >= base + WINDOW).astype(jnp.float32), axis=0, keepdims=True)
        beyond.append(jnp.broadcast_to(over, (1, 128)))
    spare = jnp.zeros((8 - 3 * STEPS, 128), jnp.float32)
    edge_ref[...] = jnp.concatenate(lines + beyond + [spare], axis=0).astype(jnp.int32)


def products(t, i, base, window, keep, high_ref, low_ref, cell_ref):
    row_iota = lax.broadcasted_iota(jnp.int32, (window, CHUNK), 0) + base
    col_iota = lax.broadcasted_iota(jnp.int32, (CB, CHUNK), 0)
    cell = cell_ref[t, 0, pl.ds(i, 1), :].astype(jnp.int32)
    col_hot = (col_iota == (cell & (CB - 1))).astype(jnp.float32).astype(BF)
    hit = row_iota == (cell >> 8)
    if keep is not None:
        hit = hit & (row_iota >= keep)
    row_hot = hit.astype(jnp.float32).astype(BF)
    lhs = jnp.concatenate([row_hot * ref[t, k, pl.ds(i, 1), :].astype(BF) for ref in (high_ref, low_ref) for k in range(VALS)], axis=0)
    out = lax.dot_general(lhs, col_hot, NT, preferred_element_type=jnp.float32)
    return out[: VALS * window] + out[VALS * window :]


def spread_step(t, chunks_from, chunks_to, window, unroll, high_ref, low_ref, cell_ref, edge_ref, acc_ref):
    def gain(base, out):
        for k in range(VALS):
            acc_ref[k, pl.ds(base, window), :] += out[k * window : (k + 1) * window]

    def first(i):
        return pl.multiple_of(jnp.minimum((edge_ref[2 * t, i] >> 3) << 3, CA - window), 8)

    def body(j, carry):
        chunks = [j * unroll + u for u in range(unroll)]
        bases = [first(i) for i in chunks]
        outs = [products(t, i, base, window, None, high_ref, low_ref, cell_ref) for i, base in zip(chunks, bases)]
        for base, out in zip(bases, outs):
            gain(base, out)
        return carry

    lax.fori_loop(chunks_from // unroll, chunks_to // unroll, body, 0)

    def rest(i, carry):
        def more(start):
            base = pl.multiple_of(jnp.minimum(start, CA - window), 8)
            gain(base, products(t, i, base, window, start, high_ref, low_ref, cell_ref))
            return start + window

        lax.while_loop(lambda start: start <= edge_ref[2 * t + 1, i], more, first(i) + window)
        return carry

    last = jnp.where(edge_ref[2 * STEPS + t, 0] > 0, chunks_to, chunks_from)
    lax.fori_loop(chunks_from, last, rest, 0)


def row_lines(plane, count, top_ref, bottom_ref):
    for p in range(count):
        top_ref[p : p + 1, :] = plane(p, pl.ds(0, 8), pl.ds(0, CB))[:1]
        bottom_ref[p : p + 1, :] = plane(p, pl.ds(CA - 8, 8), pl.ds(0, CB))[7:]


def column_lines(plane, count):
    lane = lax.broadcasted_iota(jnp.int32, (CA, 128), 1)
    picked = jnp.zeros((CA, 128), jnp.float32)
    for p in range(count):
        picked = jnp.where(lane == p, plane(p, pl.ds(0, CA), pl.ds(0, 128))[:, :1], picked)
        picked = jnp.where(lane == count + p, plane(p, pl.ds(0, CA), pl.ds(CB - 128, 128))[:, 127:], picked)
    lines = picked.T
    return lines[:count], lines[count : 2 * count]


def swapped(x, axis, odd):
    count = lax.axis_size(axis)
    pairs = [(i, (i + 1) % count) for i in range(odd, count, 2)]
    return lax.ppermute(x, axis, pairs + [(j, i) for i, j in pairs])


def after(x, *others):
    return lax.optimization_barrier((x, *others))


FRAME = PLANES + 2 * LEV


def per_plane(levels):
    return jnp.concatenate([levels] * FIELDS, axis=0)


def write_frame(plane, mix_h_ref, courant_ref, frame_ref):
    columns = column_lines(plane, PLANES)
    mix = column_lines(lambda k, rows, cols: mix_h_ref[k, rows, cols], LEV)
    along = column_lines(lambda k, rows, cols: courant_ref[0, k, rows, cols], LEV)
    across = column_lines(lambda k, rows, cols: courant_ref[1, k, rows, cols], LEV)
    place = lax.broadcasted_iota(jnp.int32, (LEV, CA), 1)
    for n, sign in ((0, -0.5), (1, 0.5)):
        ends = jnp.where(place == 0, mix[n] - 0.5 * along[n], jnp.where(place == CA - 1, mix[n] + 0.5 * along[n], 0.0))
        frame_ref[2 * FRAME : 3 * FRAME, n * CA : (n + 1) * CA] = jnp.concatenate([columns[n], mix[n] + sign * across[n], ends], axis=0)
    place = lax.broadcasted_iota(jnp.int32, (LEV, CB), 1)
    for n, sign, at in ((0, -0.5, 0), (1, 0.5, 7)):
        rows = pl.ds((CA - 8) * n, 8)

        def line(read, count):
            return jnp.concatenate([read(k, rows, pl.ds(0, CB))[at : at + 1] for k in range(count)], axis=0)

        mix = line(lambda k, rows, cols: mix_h_ref[k, rows, cols], LEV)
        along = line(lambda k, rows, cols: courant_ref[0, k, rows, cols], LEV)
        across = line(lambda k, rows, cols: courant_ref[1, k, rows, cols], LEV)
        ends = jnp.where(place == 0, mix - 0.5 * across, jnp.where(place == CB - 1, mix + 0.5 * across, 0.0))
        frame_ref[n * FRAME : (n + 1) * FRAME, :] = jnp.concatenate([line(plane, PLANES), mix + sign * along, ends], axis=0)


def ends_of(length, first, final):
    place = lax.broadcasted_iota(jnp.int32, (PLANES, length), 1)
    return jnp.where(place == 0, first, jnp.where(place == length - 1, final, 0.0))


def beside(sent, own, corners):
    edge, factor, ends = sent[:PLANES], sent[2 * PLANES : 2 * PLANES + LEV], sent[2 * PLANES + LEV :]
    return edge + per_plane(factor) * own[:PLANES] + per_plane(ends) * corners


def gained(sent, own):
    return per_plane(own[PLANES : PLANES + LEV]) * sent[PLANES : 2 * PLANES]


def step_kernel(last, *refs):
    half = PLANES // 2
    if last:
        ts_any, uv_any, mix_h_ref, mix_v_ref, courant_ref, turn_ref, *sent_refs, frame_ref, corner_ref, forcing_ref, out_any, state_ref, column_ref, out_ref, sem, out_sem = refs
        uv_any_half = uv_any
    else:
        ts_any, mix_h_any, mix_v_any, courant_any, turn_any, ts_out, uv_out, frame_any = refs[:8]
        state_ref, mix_h_ref, mix_v_ref, courant_ref, turn_ref, frame_ref, out_ref, sem, out_sem = refs[8:]
        uv_any_half = ts_any.at[pl.ds(half, half)]
    pairs = [(ts_any.at[pl.ds(0, half)], state_ref.at[pl.ds(0, half), pl.ds(8, CA)]), (uv_any_half, state_ref.at[pl.ds(half, half), pl.ds(8, CA)])]
    if not last:
        pairs += [(mix_h_any, mix_h_ref), (mix_v_any, mix_v_ref), (courant_any, courant_ref), (turn_any, turn_ref)]
    loads = [pltpu.make_async_copy(x, y, sem.at[n]) for n, (x, y) in enumerate(pairs)]
    for load in loads:
        load.start()
    if last:
        tx, ty = lax.axis_index("tx"), lax.axis_index("ty")
        there = tx > 0, tx < lax.axis_size("tx") - 1, ty > 0, ty < lax.axis_size("ty") - 1
        sent = []
        for place, even_ref, odd_ref in ((tx, *sent_refs[:2]), (ty, *sent_refs[2:])):
            even, odd = even_ref[...], odd_ref[...]
            is_odd = lax.rem(place, 2) == 1
            sent += [jnp.where(is_odd, even, odd), jnp.where(is_odd, odd, even)]
        before, after, prior, next_ = [jnp.where(flag, x, 0.0) for x, flag in zip(sent, there)]
        top, bottom = frame_ref[:FRAME], frame_ref[FRAME : 2 * FRAME]
        left, right = frame_ref[2 * FRAME : 3 * FRAME, :CA], frame_ref[2 * FRAME : 3 * FRAME, CA:]
        corner = [corner_ref[:, c : c + 1] for c in range(4)]
        beside_prior = beside(prior, left, ends_of(CA, corner[3], corner[1]))
        beside_next = beside(next_, right, ends_of(CA, corner[2], corner[0]))
        spare = jnp.zeros((128 - 4 * PLANES, CA), jnp.float32)
        column_ref[...] = jnp.concatenate([beside_prior, beside_next, gained(prior, left), gained(next_, right), spare], axis=0).T
        beside_before = beside(before, top, ends_of(CB, corner[3], corner[2]))
        beside_after = beside(after, bottom, ends_of(CB, corner[1], corner[0]))
        gain_before, gain_after = gained(before, top), gained(after, bottom)
        for p in range(PLANES):
            state_ref[p, 0:8, :] = jnp.broadcast_to(beside_before[p : p + 1, :], (8, CB))
            state_ref[p, CA + 8 : CA + 16, :] = jnp.broadcast_to(beside_after[p : p + 1, :], (8, CB))
    else:
        state_ref[:, 0:8, :] = jnp.zeros((PLANES, 8, CB), jnp.float32)
        state_ref[:, CA + 8 : CA + 16, :] = jnp.zeros((PLANES, 8, CB), jnp.float32)
    for load in loads:
        load.wait()
    if last:
        edge = lax.broadcasted_iota(jnp.int32, (CA, 128), 1)
        for p in range(PLANES):
            for lanes, at, n in ((pl.ds(0, 128), 0, 2), (pl.ds(CB - 128, 128), 127, 3)):
                gain = column_ref[:, n * PLANES + p : n * PLANES + p + 1]
                state_ref[p, pl.ds(8, CA), lanes] += jnp.where(edge == at, gain, 0.0)
            state_ref[p, 8:9, :] += gain_before[p : p + 1, :]
            state_ref[p, CA + 7 : CA + 8, :] += gain_after[p : p + 1, :]
    else:
        write_frame(lambda p, rows, cols: state_ref[p, pl.ds(8 + rows.start, rows.size), cols], mix_h_ref, courant_ref, frame_ref)
    sub = lax.broadcasted_iota(jnp.int32, (8, CB), 0)
    lane = lax.broadcasted_iota(jnp.int32, (8, CB), 1)

    def store_of(i):
        rows = pl.ds(pl.multiple_of(i * 8, 8), 8)
        if last:
            return [pltpu.make_async_copy(out_ref.at[:, rows], out_any.at[:, rows], out_sem.at[0, i])]
        parts = (pl.ds(0, half), ts_out), (pl.ds(half, half), uv_out)
        return [pltpu.make_async_copy(out_ref.at[planes, rows], out.at[:, rows], out_sem.at[n, i]) for n, (planes, out) in enumerate(parts)]

    def strip(i, carry):
        at = pl.multiple_of(i * 8, 8)
        rows = pl.ds(at, 8)
        sides = column_ref[rows, :] if last else None
        turn = turn_ref[rows, :]
        mix_v = [mix_v_ref[k, rows, :] for k in range(LEV - 1)]
        centre = [state_ref[p, pl.ds(at + 8, 8), :] for p in range(PLANES)]
        for k in range(LEV):
            mix_h = mix_h_ref[k, rows, :]
            c0 = 0.5 * courant_ref[0, k, rows, :]
            c1 = 0.5 * courant_ref[1, k, rows, :]
            for f in range(FIELDS):
                p = f * LEV + k
                a = centre[p]
                below = state_ref[p, rows, :]
                above = state_ref[p, pl.ds(at + 16, 8), :]
                up = jnp.where(sub == 7, pltpu.roll(above, 7, 0), pltpu.roll(a, 7, 0))
                down = jnp.where(sub == 0, pltpu.roll(below, 1, 0), pltpu.roll(a, 1, 0))
                right = jnp.where(lane == CB - 1, sides[:, PLANES + p : PLANES + p + 1] if last else 0.0, pltpu.roll(a, CB - 1, 1))
                left = jnp.where(lane == 0, sides[:, p : p + 1] if last else 0.0, pltpu.roll(a, 1, 1))
                new = a + mix_h * (up + down + right + left - 4.0 * a) + c0 * (up - down) + c1 * (right - left)
                if k < LEV - 1:
                    new = new + mix_v[k] * (centre[p + 1] - a)
                if k > 0:
                    new = new - mix_v[k - 1] * (a - centre[p - 1])
                if f == 2:
                    new = new + turn * centre[p + LEV]
                if f == 3:
                    new = new - turn * centre[p - LEV]
                if last and f < 2:
                    new = new + forcing_ref[p, rows, :]
                out_ref[p, rows, :] = new
        for store in store_of(i):
            store.start()
        return carry

    def finish(i, carry):
        for store in store_of(i):
            store.wait()
        return carry

    lax.fori_loop(0, CA // 8, strip, 0, unroll=4)
    if not last:

        def plane(p, rows, cols):
            return out_ref[half + p, rows, cols]

        at = 3 * FRAME
        row_lines(plane, half, frame_ref.at[pl.ds(at, half)], frame_ref.at[pl.ds(at + half, half)])
        frame_ref[at + PLANES :, :CA], frame_ref[at + PLANES :, CA:] = column_lines(plane, half)
        frame_store = pltpu.make_async_copy(frame_ref, frame_any, sem.at[6])
        frame_store.start()
    lax.fori_loop(0, CA // 8, finish, 0)
    if not last:
        frame_store.wait()


HALF = jax.ShapeDtypeStruct((PLANES // 2, CA, CB), jnp.float32)


def first_step(state, coefficients):
    frame = jax.ShapeDtypeStruct((3 * FRAME + PLANES + PLANES // 2, CB), jnp.float32)
    scratch = [pltpu.VMEM((PLANES, CA + 16, CB), jnp.float32)] + [pltpu.VMEM(x.shape, jnp.float32) for x in (*coefficients, frame)]
    scratch += [pltpu.VMEM((PLANES, CA, CB), jnp.float32), pltpu.SemaphoreType.DMA((8,)), pltpu.SemaphoreType.DMA((2, CA // 8))]
    return pl.pallas_call(
        functools.partial(step_kernel, False),
        out_shape=(HALF, HALF, frame),
        in_specs=[ANYWHERE] * 5,
        out_specs=[ANYWHERE] * 3,
        scratch_shapes=scratch,
        compiler_params=FULL,
        name="first_step",
    )(state, *coefficients)


def last_step(ts, uv, coefficients, sent, frame, corners, forcing):
    scratch = [pltpu.VMEM((PLANES, CA + 16, CB), jnp.float32), pltpu.VMEM((CA, 128), jnp.float32)]
    scratch += [pltpu.VMEM((PLANES, CA, CB), jnp.float32), pltpu.SemaphoreType.DMA((2,)), pltpu.SemaphoreType.DMA((1, CA // 8))]
    return pl.pallas_call(
        functools.partial(step_kernel, True),
        out_shape=jax.ShapeDtypeStruct((PLANES, CA, CB), jnp.float32),
        in_specs=[ANYWHERE] * 2 + [WHOLE] * 11,
        out_specs=ANYWHERE,
        scratch_shapes=scratch,
        compiler_params=STEP,
        name="last_step",
    )(ts, uv, *coefficients, *sent, frame, corners, forcing)


LISTS = (
    jax.ShapeDtypeStruct((STEPS, VALS, 32, CHUNK), jnp.float32),
    jax.ShapeDtypeStruct((STEPS, VALS, 32, CHUNK), jnp.float32),
    jax.ShapeDtypeStruct((STEPS, 1, 32, CHUNK), jnp.float32),
    jax.ShapeDtypeStruct((8, 128), jnp.int32),
)
WINDOW, UNROLL = 32, 16


def corner_columns(got_ref):
    tx, ty = lax.axis_index("tx"), lax.axis_index("ty")
    rows, columns = lax.axis_size("tx"), lax.axis_size("ty")
    plane = lax.broadcasted_iota(jnp.int32, (PLANES, 128), 0)
    lane = lax.broadcasted_iota(jnp.int32, (PLANES, 128), 1)
    out = jnp.zeros((PLANES, 128), jnp.float32)
    for c, (x, y) in enumerate(((1, 1), (1, -1), (-1, 1), (-1, -1))):
        there = (tx + x >= 0) & (tx + x < rows) & (ty + y >= 0) & (ty + y < columns)
        source = jnp.where(there, (tx + x) * columns + ty + y, 0)
        row = got_ref[pl.ds(source * WIRE + WORDS, 1), :]
        picked = jnp.sum(jnp.where(lane == plane + c * PLANES, row, 0.0), axis=1, keepdims=True)
        out = jnp.where((lane == c) & there, picked, out)
    return out


def first_records_kernel(got_ref, still_any, frame_any, ts_ref, high_ref, low_ref, cell_ref, edge_ref, corner_ref, top_ref, bottom_ref, left_ref, right_ref, frame_ref, smem_ref, sem):
    pairs = (still_any, ts_ref), (frame_any, frame_ref)
    loads = [pltpu.make_async_copy(x, y, sem.at[n]) for n, (x, y) in enumerate(pairs)]
    for load in loads:
        load.start()
    order_kernel(got_ref, high_ref, low_ref, cell_ref)
    bounds_of(cell_ref, edge_ref)
    copy = pltpu.make_async_copy(edge_ref, smem_ref, sem.at[2])
    copy.start()
    corner_ref[...] = corner_columns(got_ref)
    for load in loads:
        load.wait()
    copy.wait()
    half = PLANES // 2
    spread_step(0, 0, 32, WINDOW, UNROLL, high_ref, low_ref, cell_ref, smem_ref, ts_ref)

    def plane(p, rows, cols):
        return ts_ref[p, rows, cols]

    at = 3 * FRAME
    lines, sides = [], []
    columns = column_lines(plane, half)
    for n in range(2):
        rows = pl.ds((CA - 8) * n, 8)
        edge = [plane(p, rows, pl.ds(0, CB))[7 * n : 7 * n + 1] for p in range(half)]
        lines.append(jnp.concatenate(edge + [frame_ref[at + n * half : at + (n + 1) * half, :], frame_ref[n * FRAME : (n + 1) * FRAME, :]], axis=0))
        lanes = slice(n * CA, (n + 1) * CA)
        sides.append(jnp.concatenate([columns[n], frame_ref[at + PLANES :, lanes], frame_ref[2 * FRAME : 3 * FRAME, lanes]], axis=0))
    for axis, (first, final), even_ref, odd_ref in (("tx", lines, top_ref, bottom_ref), ("ty", sides, left_ref, right_ref)):
        odd = lax.rem(lax.axis_index(axis), 2) == 1
        even_ref[...] = jnp.where(odd, first, final)
        odd_ref[...] = jnp.where(odd, final, first)


EDGES = (jax.ShapeDtypeStruct((PLANES + FRAME, CB), jnp.float32),) * 2 + (jax.ShapeDtypeStruct((PLANES + FRAME, CA), jnp.float32),) * 2


def first_records(got, still, frame):
    out = pl.pallas_call(
        first_records_kernel,
        out_shape=(HALF,) + LISTS + (jax.ShapeDtypeStruct((PLANES, 128), jnp.float32),) + EDGES,
        in_specs=[WHOLE, ANYWHERE, ANYWHERE],
        out_specs=[WHOLE] * 10,
        scratch_shapes=[
            pltpu.VMEM(frame.shape, jnp.float32),
            pltpu.SMEM((8, 128), jnp.int32),
            pltpu.SemaphoreType.DMA((3,)),
        ],
        compiler_params=PARAMS,
        name="first_records",
    )(got, still, frame)
    return out[0], out[1:5], out[5], out[6:]


def second_records_kernel(high_ref, low_ref, cell_ref, edge_ref, out_ref):
    out_ref[...] = jnp.zeros_like(out_ref)
    spread_step(1, 0, 32, WINDOW, UNROLL, high_ref, low_ref, cell_ref, edge_ref, out_ref)


def second_records(lists):
    return pl.pallas_call(
        second_records_kernel,
        out_shape=HALF,
        in_specs=[WHOLE] * 3 + [pl.BlockSpec(memory_space=pltpu.SMEM)],
        out_specs=WHOLE,
        compiler_params=PARAMS,
        name="second_records",
    )(*lists)


def local(adjoint_start, mixing_h, mixing_v, courant, coriolis, misfit, owner, column):
    devices = lax.axis_size("tx") * lax.axis_size("ty")
    state = adjoint_start.reshape(PLANES, CA, CB)
    coefficients = (mixing_h, mixing_v, courant, coriolis)
    sent = pack(owner.transpose(0, 2, 1), column, misfit, state, devices)
    got = lax.all_to_all(sent.reshape(devices, 1, WIRE * 128), ("tx", "ty"), split_axis=0, concat_axis=0, tiled=True)
    still, uv, frame = first_step(state, coefficients)
    ts, lists, corners, edges = first_records(got.reshape(devices * WIRE, 128), still, frame)
    x0 = swapped(edges[0], "tx", 0)
    x1 = swapped(edges[1], "tx", 1)
    y0 = swapped(edges[2], "ty", 0)
    y1 = swapped(edges[3], "ty", 1)
    forcing = second_records(lists)
    return last_step(ts, uv, coefficients, (x0, x1, y0, y1), frame, corners, forcing).reshape(FIELDS, LEV, CA, CB)


def solution(mesh):
    return jax.shard_map(
        local,
        mesh=mesh,
        in_specs=(
            P(None, None, "tx", "ty"),
            P(None, "tx", "ty"),
            P(None, "tx", "ty"),
            P(None, None, "tx", "ty"),
            P("tx", "ty"),
            P(None, None, ("tx", "ty")),
            P(None, ("tx", "ty"), None),
            P(None, ("tx", "ty")),
        ),
        out_specs=P(None, None, "tx", "ty"),
        check_vma=False,
    )
```

```python
import functools
import jax
import jax.numpy as jnp
from jax import lax
from jax.experimental import pallas as pl
from jax.experimental.pallas import tpu as pltpu
from jax.sharding import PartitionSpec as P

CA, CB, LEV, STEPS, CAP = 128, 256, 4, 2, 64
FIELDS = 4
PLANES = FIELDS * LEV
VALS = 2 * LEV
WORDS = VALS + 1
WIRE = WORDS + 1
CHUNK = 256
BF = jnp.bfloat16
NT = (((1,), (1,)), ((), ()))
LIMIT = 24
WHOLE = pl.BlockSpec(memory_space=pltpu.VMEM)
ANYWHERE = pl.BlockSpec(memory_space=pltpu.HBM)
PARAMS = pltpu.CompilerParams(vmem_limit_bytes=LIMIT << 20)
STEP = pltpu.CompilerParams(vmem_limit_bytes=40 << 20)
FULL = pltpu.CompilerParams(vmem_limit_bytes=63400000)


def halves(x):
    top = x.astype(BF)
    return top, (x - top.astype(jnp.float32)).astype(BF)


def slots(owner_ref, place_ref, devices):
    r = lax.broadcasted_iota(jnp.int32, (CHUNK, CHUNK), 0)
    c = lax.broadcasted_iota(jnp.int32, (CHUNK, CHUNK), 1)
    earlier = (r < c).astype(jnp.float32).astype(BF)
    tiles = lax.broadcasted_iota(jnp.int32, (devices, CHUNK), 0)
    counts = [jnp.zeros((devices, 1), jnp.float32)] * STEPS
    for i in range(owner_ref.shape[2] // CHUNK):
        at = pl.ds(i * CHUNK, CHUNK)
        for t in range(STEPS):
            target = owner_ref[t, :, at]
            hot = tiles == target
            ones = hot.astype(jnp.float32)
            before = jnp.dot(ones.astype(BF), earlier, preferred_element_type=jnp.float32)
            slot = jnp.sum(jnp.where(hot, before + counts[t], 0.0), axis=0, keepdims=True)
            counts[t] = counts[t] + before[:, CHUNK - 1 :] + ones[:, CHUNK - 1 :]
            place_ref[t, :, at] = (target & 3) * CAP + slot.astype(jnp.int32)


def gather(span, owner_ref, place_ref, column_ref, misfit_ref, acc_ref):
    groups = acc_ref.shape[1] // WORDS
    group_row = lax.broadcasted_iota(jnp.int32, (groups, span), 0)
    place_row = lax.broadcasted_iota(jnp.int32, (CHUNK, span), 0)

    def part(t, i):
        at = pl.ds(pl.multiple_of(i * span, span), span)
        group_hot = (group_row == (owner_ref[t, :, at] >> 2)).astype(jnp.float32).astype(BF)
        place_hot = (place_row == place_ref[t, :, at]).astype(jnp.float32).astype(BF)
        cell = column_ref[t : t + 1, at]
        high, low = halves(misfit_ref[t, :, at])
        row = (cell - (cell & (CB - 1))).astype(jnp.float32).astype(BF)
        col = ((cell & (CB - 1)) + 1).astype(jnp.float32).astype(BF)
        lhs_h = jnp.concatenate([group_hot * high[k : k + 1] for k in range(VALS)] + [group_hot * row], axis=0)
        lhs_l = jnp.concatenate([group_hot * low[k : k + 1] for k in range(VALS)] + [group_hot * col], axis=0)
        lhs = jnp.concatenate([lhs_h, lhs_l], axis=1)
        rhs = jnp.concatenate([place_hot, place_hot], axis=1)
        return lax.dot_general(lhs, rhs, NT, preferred_element_type=jnp.float32)

    def body(i, carry):
        for t in range(STEPS):
            acc_ref[t] += part(t, i)
        return carry

    for t in range(STEPS):
        acc_ref[t] = part(t, 0)
    lax.fori_loop(1, owner_ref.shape[2] // span, body, 0)


def corner_row(first, final):
    plane = lax.broadcasted_iota(jnp.int32, (PLANES, 128), 0)
    lane = lax.broadcasted_iota(jnp.int32, (PLANES, 128), 1)
    row = jnp.zeros((PLANES, 128), jnp.float32)
    for c, x in enumerate((first[:, :1], first[:, CB - 1 :], final[:, :1], final[:, CB - 1 :])):
        row = jnp.where(lane == plane + c * PLANES, x, row)
    return jnp.sum(row, axis=0, keepdims=True)


def pack_kernel(devices, span, owner_any, column_any, misfit_any, state_any, out_any, owner_ref, column_ref, misfit_ref, place_ref, acc_ref, out_ref, tile_ref, sem):
    pairs = [(owner_any, owner_ref), (column_any, column_ref), (misfit_any, misfit_ref)]
    pairs += [(state_any.at[:, pl.ds(at, 8)], tile_ref.at[n]) for n, at in enumerate((0, CA - 8))]
    loads = [pltpu.make_async_copy(x, y, sem.at[n]) for n, (x, y) in enumerate(pairs)]
    for load in loads:
        load.start()
    loads[0].wait()
    slots(owner_ref, place_ref, devices)
    for load in loads[1:]:
        load.wait()
    first = jnp.concatenate([tile_ref[0, p, :1, :] for p in range(PLANES)], axis=0)
    final = jnp.concatenate([tile_ref[1, p, 7:, :] for p in range(PLANES)], axis=0)
    out_ref[pl.ds(WORDS, devices, stride=WIRE), :] = jnp.broadcast_to(corner_row(first, final), (devices, 128))
    gather(span, owner_ref, place_ref, column_ref, misfit_ref, acc_ref)
    groups = devices // 4
    left = lax.broadcasted_iota(jnp.int32, (groups // 2, 128), 1) < CAP
    half = groups // 2
    stores = []
    for part in range(2):
        start = part * half * 4 * WIRE
        for k in range(WORDS):
            for j in range(2):
                a = acc_ref[0, pl.ds(k * groups + part * half, half), pl.ds(j * 128, 128)]
                b = acc_ref[1, pl.ds(k * groups + part * half, half), pl.ds(j * 128, 128)]
                out_ref[pl.ds(start + 2 * j * WIRE + k, half, stride=4 * WIRE), :] = jnp.where(left, a, pltpu.roll(b, CAP, 1))
                out_ref[pl.ds(start + (2 * j + 1) * WIRE + k, half, stride=4 * WIRE), :] = jnp.where(left, pltpu.roll(a, CAP, 1), b)
        rows = pl.ds(start, half * 4 * WIRE)
        stores.append(pltpu.make_async_copy(out_ref.at[rows], out_any.at[rows], sem.at[5 + part]))
        stores[part].start()
    for store in stores:
        store.wait()


def pack(owner, column, misfit, state, devices, span=2048):
    sent = jax.ShapeDtypeStruct((devices * WIRE, 128), jnp.float32)
    return pl.pallas_call(
        functools.partial(pack_kernel, devices, span),
        out_shape=sent,
        in_specs=[ANYWHERE] * 4,
        out_specs=ANYWHERE,
        scratch_shapes=[
            pltpu.VMEM(owner.shape, jnp.int32),
            pltpu.VMEM(column.shape, jnp.int32),
            pltpu.VMEM(misfit.shape, jnp.float32),
            pltpu.VMEM(owner.shape, jnp.int32),
            pltpu.VMEM((STEPS, WORDS * devices // 4, CHUNK), jnp.float32),
            pltpu.VMEM(sent.shape, jnp.float32),
            pltpu.VMEM((2, PLANES, 8, CB), jnp.float32),
            pltpu.SemaphoreType.DMA((7,)),
        ],
        compiler_params=FULL,
        name="pack",
    )(owner, column, misfit, state)


def exchange(keys, span, reach, flip=None):
    sub = lax.broadcasted_iota(jnp.int32, (8, 128), 0)
    count = len(keys)
    keys = list(keys)
    if span < 8 * count:
        flip = (sub & (span // count)) != 0 if span >= count else None
    if reach < count:
        for v in range(count):
            w = v ^ reach
            if v > w:
                continue
            low, high = jnp.minimum(keys[v], keys[w]), jnp.maximum(keys[v], keys[w])
            if flip is not None:
                low, high = jnp.where(flip, high, low), jnp.where(flip, low, high)
            elif span < count and v & span:
                low, high = high, low
            keys[v], keys[w] = low, high
        return keys
    step = reach // count
    second = (sub & step) != 0
    upper = second if flip is None else second != flip
    for v in range(count):
        other = jnp.where(second, pltpu.roll(keys[v], step, 0), pltpu.roll(keys[v], 8 - step, 0))
        keys[v] = jnp.where(upper, jnp.maximum(keys[v], other), jnp.minimum(keys[v], other))
    return keys


def sort_rows(keys):
    length = 8 * len(keys)
    beyond = (lax.broadcasted_iota(jnp.int32, (8, 128), 1) & 32) != 0
    span = 2
    while span <= length:
        reach = span // 2
        while reach:
            keys = exchange(keys, span, reach, beyond)
            reach //= 2
        span *= 2
    other = [jnp.where(beyond, pltpu.roll(x, 32, 1), pltpu.roll(x, 96, 1)) for x in keys]
    keys = [jnp.where(beyond, jnp.maximum(x, y), jnp.minimum(x, y)) for x, y in zip(keys, other)]
    reach = length // 2
    while reach:
        keys = exchange(keys, length, reach)
        reach //= 2
    return keys


def order_kernel(got_ref, high_ref, low_ref, cell_ref):
    lanes = lax.broadcasted_iota(jnp.int32, (128, 128), 1)
    rows = lax.broadcasted_iota(jnp.int32, (128, 128), 0)
    left = lanes < CAP

    def list_of(k):
        a = got_ref[pl.ds(k, 64, stride=WIRE), :]
        b = got_ref[pl.ds(64 * WIRE + k, 64, stride=WIRE), :]
        first = jnp.where(left[:64], a, pltpu.roll(b, CAP, 1))
        second = jnp.where(left[:64], pltpu.roll(a, CAP, 1), b)
        return jnp.concatenate([first, second], axis=0)

    ids = list_of(VALS).astype(jnp.int32)
    slot = lanes & (CAP - 1)
    spread = ((slot & 1) << 5) | ((slot & 2) << 3) | ((slot & 4) << 1) | ((slot & 8) >> 1) | ((slot & 16) >> 3) | ((slot & 32) >> 5)
    idle = ((spread << 1) | (lanes >> 6)) << 8
    key = (jnp.where(ids > 0, ids - 1, idle) << 8) | ((rows & 32) << 2) | lanes
    turned = key.astype(jnp.float32).T
    keys = sort_rows([turned[8 * v : 8 * v + 8] for v in range(16)])
    keys = jnp.concatenate(keys, axis=0).astype(jnp.int32)
    source = (keys & 255).astype(jnp.float32).T.astype(jnp.int32)
    lane_of, beyond = source & 127, source >= 128
    block = lanes[:8] >> 5

    def place(x, store):
        for h in range(2):
            for u in range(2):
                parts = [x[8 * v : 8 * v + 8] for v in range(8 * h + 4 * u, 8 * h + 4 * u + 4)]
                for group in range(4):
                    moved = [part if j == group else pltpu.roll(part, (j - group) % 4 * 32, 1) for j, part in enumerate(parts)]
                    tile = jnp.where(block < 2, jnp.where(block == 0, moved[0], moved[1]), jnp.where(block == 2, moved[2], moved[3]))
                    store(group // 2, pl.ds(16 * (group % 2) + 8 * h, 8), pl.ds(128 * u, 128), tile)

    def store_cell(t, at, cols, tile):
        cell_ref[t, 0, at, cols] = tile

    place((keys >> 8).astype(jnp.float32), store_cell)
    for k in range(VALS):
        x = list_of(k)
        near = jnp.concatenate([x[:32], x[:32], x[64:96], x[64:96]], axis=0)
        far = jnp.concatenate([x[32:64], x[32:64], x[96:], x[96:]], axis=0)
        picked = jnp.where(beyond, jnp.take_along_axis(far, lane_of, axis=1), jnp.take_along_axis(near, lane_of, axis=1))

        def store_value(t, at, cols, tile, k=k):
            top = tile.astype(BF).astype(jnp.float32)
            high_ref[t, k, at, cols] = top
            low_ref[t, k, at, cols] = tile - top

        place(picked.T, store_value)


def bounds_of(cell_ref, edge_ref):
    chunk = lax.broadcasted_iota(jnp.int32, (32, 128), 0)
    lane = lax.broadcasted_iota(jnp.int32, (32, 128), 1)
    lines, beyond = [], []
    for t in range(STEPS):
        row = cell_ref[t, 0].astype(jnp.int32) >> 8
        least = jnp.min(jnp.minimum(row[:, :128], row[:, 128:]).astype(jnp.float32), axis=1, keepdims=True)
        most = jnp.max(jnp.maximum(row[:, :128], row[:, 128:]).astype(jnp.float32), axis=1, keepdims=True)
        lines += [jnp.sum(jnp.where(chunk == lane, e, 0.0), axis=0, keepdims=True) for e in (least, most)]
        base = jnp.minimum((least.astype(jnp.int32) >> 3) << 3, CA - WINDOW)
        over = jnp.max((most.astype(jnp.int32) >= base + WINDOW).astype(jnp.float32), axis=0, keepdims=True)
        beyond.append(jnp.broadcast_to(over, (1, 128)))
    spare = jnp.zeros((8 - 3 * STEPS, 128), jnp.float32)
    edge_ref[...] = jnp.concatenate(lines + beyond + [spare], axis=0).astype(jnp.int32)


def products(t, i, base, window, keep, high_ref, low_ref, cell_ref):
    row_iota = lax.broadcasted_iota(jnp.int32, (window, CHUNK), 0) + base
    col_iota = lax.broadcasted_iota(jnp.int32, (CB, CHUNK), 0)
    cell = cell_ref[t, 0, pl.ds(i, 1), :].astype(jnp.int32)
    col_hot = (col_iota == (cell & (CB - 1))).astype(jnp.float32).astype(BF)
    hit = row_iota == (cell >> 8)
    if keep is not None:
        hit = hit & (row_iota >= keep)
    row_hot = hit.astype(jnp.float32).astype(BF)
    lhs = jnp.concatenate([row_hot * ref[t, k, pl.ds(i, 1), :].astype(BF) for ref in (high_ref, low_ref) for k in range(VALS)], axis=0)
    out = lax.dot_general(lhs, col_hot, NT, preferred_element_type=jnp.float32)
    return out[: VALS * window] + out[VALS * window :]


def spread_step(t, chunks_from, chunks_to, window, unroll, high_ref, low_ref, cell_ref, edge_ref, acc_ref):
    def gain(base, out):
        for k in range(VALS):
            acc_ref[k, pl.ds(base, window), :] += out[k * window : (k + 1) * window]

    def first(i):
        return pl.multiple_of(jnp.minimum((edge_ref[2 * t, i] >> 3) << 3, CA - window), 8)

    def body(j, carry):
        chunks = [j * unroll + u for u in range(unroll)]
        bases = [first(i) for i in chunks]
        outs = [products(t, i, base, window, None, high_ref, low_ref, cell_ref) for i, base in zip(chunks, bases)]
        for base, out in zip(bases, outs):
            gain(base, out)
        return carry

    lax.fori_loop(chunks_from // unroll, chunks_to // unroll, body, 0)

    def rest(i, carry):
        def more(start):
            base = pl.multiple_of(jnp.minimum(start, CA - window), 8)
            gain(base, products(t, i, base, window, start, high_ref, low_ref, cell_ref))
            return start + window

        lax.while_loop(lambda start: start <= edge_ref[2 * t + 1, i], more, first(i) + window)
        return carry

    last = jnp.where(edge_ref[2 * STEPS + t, 0] > 0, chunks_to, chunks_from)
    lax.fori_loop(chunks_from, last, rest, 0)


def row_lines(plane, count, top_ref, bottom_ref):
    for p in range(count):
        top_ref[p : p + 1, :] = plane(p, pl.ds(0, 8), pl.ds(0, CB))[:1]
        bottom_ref[p : p + 1, :] = plane(p, pl.ds(CA - 8, 8), pl.ds(0, CB))[7:]


def column_lines(plane, count):
    lane = lax.broadcasted_iota(jnp.int32, (CA, 128), 1)
    picked = jnp.zeros((CA, 128), jnp.float32)
    for p in range(count):
        picked = jnp.where(lane == p, plane(p, pl.ds(0, CA), pl.ds(0, 128))[:, :1], picked)
        picked = jnp.where(lane == count + p, plane(p, pl.ds(0, CA), pl.ds(CB - 128, 128))[:, 127:], picked)
    lines = picked.T
    return lines[:count], lines[count : 2 * count]


def swapped(x, axis, odd):
    count = lax.axis_size(axis)
    pairs = [(i, (i + 1) % count) for i in range(odd, count, 2)]
    return lax.ppermute(x, axis, pairs + [(j, i) for i, j in pairs])


def after(x, *others):
    return lax.optimization_barrier((x, *others))


FRAME = PLANES + 2 * LEV


def per_plane(levels):
    return jnp.concatenate([levels] * FIELDS, axis=0)


def write_frame(plane, mix_h_ref, courant_ref, frame_ref):
    columns = column_lines(plane, PLANES)
    mix = column_lines(lambda k, rows, cols: mix_h_ref[k, rows, cols], LEV)
    along = column_lines(lambda k, rows, cols: courant_ref[0, k, rows, cols], LEV)
    across = column_lines(lambda k, rows, cols: courant_ref[1, k, rows, cols], LEV)
    place = lax.broadcasted_iota(jnp.int32, (LEV, CA), 1)
    for n, sign in ((0, -0.5), (1, 0.5)):
        ends = jnp.where(place == 0, mix[n] - 0.5 * along[n], jnp.where(place == CA - 1, mix[n] + 0.5 * along[n], 0.0))
        frame_ref[2 * FRAME : 3 * FRAME, n * CA : (n + 1) * CA] = jnp.concatenate([columns[n], mix[n] + sign * across[n], ends], axis=0)
    place = lax.broadcasted_iota(jnp.int32, (LEV, CB), 1)
    for n, sign, at in ((0, -0.5, 0), (1, 0.5, 7)):
        rows = pl.ds((CA - 8) * n, 8)

        def line(read, count):
            return jnp.concatenate([read(k, rows, pl.ds(0, CB))[at : at + 1] for k in range(count)], axis=0)

        mix = line(lambda k, rows, cols: mix_h_ref[k, rows, cols], LEV)
        along = line(lambda k, rows, cols: courant_ref[0, k, rows, cols], LEV)
        across = line(lambda k, rows, cols: courant_ref[1, k, rows, cols], LEV)
        ends = jnp.where(place == 0, mix - 0.5 * across, jnp.where(place == CB - 1, mix + 0.5 * across, 0.0))
        frame_ref[n * FRAME : (n + 1) * FRAME, :] = jnp.concatenate([line(plane, PLANES), mix + sign * along, ends], axis=0)


def ends_of(length, first, final):
    place = lax.broadcasted_iota(jnp.int32, (PLANES, length), 1)
    return jnp.where(place == 0, first, jnp.where(place == length - 1, final, 0.0))


def beside(sent, own, corners):
    edge, factor, ends = sent[:PLANES], sent[2 * PLANES : 2 * PLANES + LEV], sent[2 * PLANES + LEV :]
    return edge + per_plane(factor) * own[:PLANES] + per_plane(ends) * corners


def gained(sent, own):
    return per_plane(own[PLANES : PLANES + LEV]) * sent[PLANES : 2 * PLANES]


def step_kernel(last, *refs):
    half = PLANES // 2
    if last:
        ts_any, uv_any, mix_h_ref, mix_v_ref, courant_ref, turn_ref, *sent_refs, frame_ref, corner_ref, forcing_ref, out_any, state_ref, column_ref, out_ref, sem, out_sem = refs
        uv_any_half = uv_any
    else:
        ts_any, mix_h_any, mix_v_any, courant_any, turn_any, ts_out, uv_out, frame_any = refs[:8]
        state_ref, mix_h_ref, mix_v_ref, courant_ref, turn_ref, frame_ref, out_ref, sem, out_sem = refs[8:]
        uv_any_half = ts_any.at[pl.ds(half, half)]
    pairs = [(ts_any.at[pl.ds(0, half)], state_ref.at[pl.ds(0, half), pl.ds(8, CA)]), (uv_any_half, state_ref.at[pl.ds(half, half), pl.ds(8, CA)])]
    if not last:
        pairs += [(mix_h_any, mix_h_ref), (mix_v_any, mix_v_ref), (courant_any, courant_ref), (turn_any, turn_ref)]
    loads = [pltpu.make_async_copy(x, y, sem.at[n]) for n, (x, y) in enumerate(pairs)]
    for load in loads:
        load.start()
    if last:
        tx, ty = lax.axis_index("tx"), lax.axis_index("ty")
        there = tx > 0, tx < lax.axis_size("tx") - 1, ty > 0, ty < lax.axis_size("ty") - 1
        sent = []
        for place, even_ref, odd_ref in ((tx, *sent_refs[:2]), (ty, *sent_refs[2:])):
            even, odd = even_ref[...], odd_ref[...]
            is_odd = lax.rem(place, 2) == 1
            sent += [jnp.where(is_odd, even, odd), jnp.where(is_odd, odd, even)]
        before, after, prior, next_ = [jnp.where(flag, x, 0.0) for x, flag in zip(sent, there)]
        top, bottom = frame_ref[:FRAME], frame_ref[FRAME : 2 * FRAME]
        left, right = frame_ref[2 * FRAME : 3 * FRAME, :CA], frame_ref[2 * FRAME : 3 * FRAME, CA:]
        corner = [corner_ref[:, c : c + 1] for c in range(4)]
        beside_prior = beside(prior, left, ends_of(CA, corner[3], corner[1]))
        beside_next = beside(next_, right, ends_of(CA, corner[2], corner[0]))
        spare = jnp.zeros((128 - 4 * PLANES, CA), jnp.float32)
        column_ref[...] = jnp.concatenate([beside_prior, beside_next, gained(prior, left), gained(next_, right), spare], axis=0).T
        beside_before = beside(before, top, ends_of(CB, corner[3], corner[2]))
        beside_after = beside(after, bottom, ends_of(CB, corner[1], corner[0]))
        gain_before, gain_after = gained(before, top), gained(after, bottom)
        for p in range(PLANES):
            state_ref[p, 0:8, :] = jnp.broadcast_to(beside_before[p : p + 1, :], (8, CB))
            state_ref[p, CA + 8 : CA + 16, :] = jnp.broadcast_to(beside_after[p : p + 1, :], (8, CB))
    else:
        state_ref[:, 0:8, :] = jnp.zeros((PLANES, 8, CB), jnp.float32)
        state_ref[:, CA + 8 : CA + 16, :] = jnp.zeros((PLANES, 8, CB), jnp.float32)
    for load in loads:
        load.wait()
    if last:
        edge = lax.broadcasted_iota(jnp.int32, (CA, 128), 1)
        for p in range(PLANES):
            for lanes, at, n in ((pl.ds(0, 128), 0, 2), (pl.ds(CB - 128, 128), 127, 3)):
                gain = column_ref[:, n * PLANES + p : n * PLANES + p + 1]
                state_ref[p, pl.ds(8, CA), lanes] += jnp.where(edge == at, gain, 0.0)
            state_ref[p, 8:9, :] += gain_before[p : p + 1, :]
            state_ref[p, CA + 7 : CA + 8, :] += gain_after[p : p + 1, :]
    else:
        write_frame(lambda p, rows, cols: state_ref[p, pl.ds(8 + rows.start, rows.size), cols], mix_h_ref, courant_ref, frame_ref)
    sub = lax.broadcasted_iota(jnp.int32, (8, CB), 0)
    lane = lax.broadcasted_iota(jnp.int32, (8, CB), 1)

    def store_of(i):
        rows = pl.ds(pl.multiple_of(i * 8, 8), 8)
        if last:
            return [pltpu.make_async_copy(out_ref.at[:, rows], out_any.at[:, rows], out_sem.at[0, i])]
        parts = (pl.ds(0, half), ts_out), (pl.ds(half, half), uv_out)
        return [pltpu.make_async_copy(out_ref.at[planes, rows], out.at[:, rows], out_sem.at[n, i]) for n, (planes, out) in enumerate(parts)]

    def strip(i, carry):
        at = pl.multiple_of(i * 8, 8)
        rows = pl.ds(at, 8)
        sides = column_ref[rows, :] if last else None
        turn = turn_ref[rows, :]
        mix_v = [mix_v_ref[k, rows, :] for k in range(LEV - 1)]
        centre = [state_ref[p, pl.ds(at + 8, 8), :] for p in range(PLANES)]
        for k in range(LEV):
            mix_h = mix_h_ref[k, rows, :]
            c0 = 0.5 * courant_ref[0, k, rows, :]
            c1 = 0.5 * courant_ref[1, k, rows, :]
            for f in range(FIELDS):
                p = f * LEV + k
                a = centre[p]
                below = state_ref[p, rows, :]
                above = state_ref[p, pl.ds(at + 16, 8), :]
                up = jnp.where(sub == 7, pltpu.roll(above, 7, 0), pltpu.roll(a, 7, 0))
                down = jnp.where(sub == 0, pltpu.roll(below, 1, 0), pltpu.roll(a, 1, 0))
                right = jnp.where(lane == CB - 1, sides[:, PLANES + p : PLANES + p + 1] if last else 0.0, pltpu.roll(a, CB - 1, 1))
                left = jnp.where(lane == 0, sides[:, p : p + 1] if last else 0.0, pltpu.roll(a, 1, 1))
                new = a + mix_h * (up + down + right + left - 4.0 * a) + c0 * (up - down) + c1 * (right - left)
                if k < LEV - 1:
                    new = new + mix_v[k] * (centre[p + 1] - a)
                if k > 0:
                    new = new - mix_v[k - 1] * (a - centre[p - 1])
                if f == 2:
                    new = new + turn * centre[p + LEV]
                if f == 3:
                    new = new - turn * centre[p - LEV]
                if last and f < 2:
                    new = new + forcing_ref[p, rows, :]
                out_ref[p, rows, :] = new
        for store in store_of(i):
            store.start()
        return carry

    def finish(i, carry):
        for store in store_of(i):
            store.wait()
        return carry

    lax.fori_loop(0, CA // 8, strip, 0, unroll=4)
    if not last:

        def plane(p, rows, cols):
            return out_ref[half + p, rows, cols]

        at = 3 * FRAME
        row_lines(plane, half, frame_ref.at[pl.ds(at, half)], frame_ref.at[pl.ds(at + half, half)])
        frame_ref[at + PLANES :, :CA], frame_ref[at + PLANES :, CA:] = column_lines(plane, half)
        frame_store = pltpu.make_async_copy(frame_ref, frame_any, sem.at[6])
        frame_store.start()
    lax.fori_loop(0, CA // 8, finish, 0)
    if not last:
        frame_store.wait()


HALF = jax.ShapeDtypeStruct((PLANES // 2, CA, CB), jnp.float32)


def first_step(state, coefficients):
    frame = jax.ShapeDtypeStruct((3 * FRAME + PLANES + PLANES // 2, CB), jnp.float32)
    scratch = [pltpu.VMEM((PLANES, CA + 16, CB), jnp.float32)] + [pltpu.VMEM(x.shape, jnp.float32) for x in (*coefficients, frame)]
    scratch += [pltpu.VMEM((PLANES, CA, CB), jnp.float32), pltpu.SemaphoreType.DMA((8,)), pltpu.SemaphoreType.DMA((2, CA // 8))]
    return pl.pallas_call(
        functools.partial(step_kernel, False),
        out_shape=(HALF, HALF, frame),
        in_specs=[ANYWHERE] * 5,
        out_specs=[ANYWHERE] * 3,
        scratch_shapes=scratch,
        compiler_params=FULL,
        name="first_step",
    )(state, *coefficients)


def last_step(ts, uv, coefficients, sent, frame, corners, forcing):
    scratch = [pltpu.VMEM((PLANES, CA + 16, CB), jnp.float32), pltpu.VMEM((CA, 128), jnp.float32)]
    scratch += [pltpu.VMEM((PLANES, CA, CB), jnp.float32), pltpu.SemaphoreType.DMA((2,)), pltpu.SemaphoreType.DMA((1, CA // 8))]
    return pl.pallas_call(
        functools.partial(step_kernel, True),
        out_shape=jax.ShapeDtypeStruct((PLANES, CA, CB), jnp.float32),
        in_specs=[ANYWHERE] * 2 + [WHOLE] * 11,
        out_specs=ANYWHERE,
        scratch_shapes=scratch,
        compiler_params=STEP,
        name="last_step",
    )(ts, uv, *coefficients, *sent, frame, corners, forcing)


LISTS = (
    jax.ShapeDtypeStruct((STEPS, VALS, 32, CHUNK), jnp.float32),
    jax.ShapeDtypeStruct((STEPS, VALS, 32, CHUNK), jnp.float32),
    jax.ShapeDtypeStruct((STEPS, 1, 32, CHUNK), jnp.float32),
    jax.ShapeDtypeStruct((8, 128), jnp.int32),
)
WINDOW, UNROLL = 32, 16


def corner_columns(got_ref):
    tx, ty = lax.axis_index("tx"), lax.axis_index("ty")
    rows, columns = lax.axis_size("tx"), lax.axis_size("ty")
    plane = lax.broadcasted_iota(jnp.int32, (PLANES, 128), 0)
    lane = lax.broadcasted_iota(jnp.int32, (PLANES, 128), 1)
    out = jnp.zeros((PLANES, 128), jnp.float32)
    for c, (x, y) in enumerate(((1, 1), (1, -1), (-1, 1), (-1, -1))):
        there = (tx + x >= 0) & (tx + x < rows) & (ty + y >= 0) & (ty + y < columns)
        source = jnp.where(there, (tx + x) * columns + ty + y, 0)
        row = got_ref[pl.ds(source * WIRE + WORDS, 1), :]
        picked = jnp.sum(jnp.where(lane == plane + c * PLANES, row, 0.0), axis=1, keepdims=True)
        out = jnp.where((lane == c) & there, picked, out)
    return out


def first_records_kernel(got_ref, still_any, frame_any, ts_ref, high_ref, low_ref, cell_ref, edge_ref, corner_ref, top_ref, bottom_ref, left_ref, right_ref, frame_ref, smem_ref, sem):
    pairs = (still_any, ts_ref), (frame_any, frame_ref)
    loads = [pltpu.make_async_copy(x, y, sem.at[n]) for n, (x, y) in enumerate(pairs)]
    for load in loads:
        load.start()
    order_kernel(got_ref, high_ref, low_ref, cell_ref)
    bounds_of(cell_ref, edge_ref)
    copy = pltpu.make_async_copy(edge_ref, smem_ref, sem.at[2])
    copy.start()
    corner_ref[...] = corner_columns(got_ref)
    for load in loads:
        load.wait()
    copy.wait()
    half = PLANES // 2
    spread_step(0, 0, 32, WINDOW, UNROLL, high_ref, low_ref, cell_ref, smem_ref, ts_ref)

    def plane(p, rows, cols):
        return ts_ref[p, rows, cols]

    at = 3 * FRAME
    lines, sides = [], []
    columns = column_lines(plane, half)
    for n in range(2):
        rows = pl.ds((CA - 8) * n, 8)
        edge = [plane(p, rows, pl.ds(0, CB))[7 * n : 7 * n + 1] for p in range(half)]
        lines.append(jnp.concatenate(edge + [frame_ref[at + n * half : at + (n + 1) * half, :], frame_ref[n * FRAME : (n + 1) * FRAME, :]], axis=0))
        lanes = slice(n * CA, (n + 1) * CA)
        sides.append(jnp.concatenate([columns[n], frame_ref[at + PLANES :, lanes], frame_ref[2 * FRAME : 3 * FRAME, lanes]], axis=0))
    for axis, (first, final), even_ref, odd_ref in (("tx", lines, top_ref, bottom_ref), ("ty", sides, left_ref, right_ref)):
        odd = lax.rem(lax.axis_index(axis), 2) == 1
        even_ref[...] = jnp.where(odd, first, final)
        odd_ref[...] = jnp.where(odd, final, first)


EDGES = (jax.ShapeDtypeStruct((PLANES + FRAME, CB), jnp.float32),) * 2 + (jax.ShapeDtypeStruct((PLANES + FRAME, CA), jnp.float32),) * 2


def first_records(got, still, frame):
    out = pl.pallas_call(
        first_records_kernel,
        out_shape=(HALF,) + LISTS + (jax.ShapeDtypeStruct((PLANES, 128), jnp.float32),) + EDGES,
        in_specs=[WHOLE, ANYWHERE, ANYWHERE],
        out_specs=[WHOLE] * 10,
        scratch_shapes=[
            pltpu.VMEM(frame.shape, jnp.float32),
            pltpu.SMEM((8, 128), jnp.int32),
            pltpu.SemaphoreType.DMA((3,)),
        ],
        compiler_params=PARAMS,
        name="first_records",
    )(got, still, frame)
    return out[0], out[1:5], out[5], out[6:]


def second_records_kernel(high_ref, low_ref, cell_ref, edge_ref, out_ref):
    out_ref[...] = jnp.zeros_like(out_ref)
    spread_step(1, 0, 32, WINDOW, UNROLL, high_ref, low_ref, cell_ref, edge_ref, out_ref)


def second_records(lists):
    return pl.pallas_call(
        second_records_kernel,
        out_shape=HALF,
        in_specs=[WHOLE] * 3 + [pl.BlockSpec(memory_space=pltpu.SMEM)],
        out_specs=WHOLE,
        compiler_params=PARAMS,
        name="second_records",
    )(*lists)


def local(adjoint_start, mixing_h, mixing_v, courant, coriolis, misfit, owner, column):
    devices = lax.axis_size("tx") * lax.axis_size("ty")
    state = adjoint_start.reshape(PLANES, CA, CB)
    coefficients = (mixing_h, mixing_v, courant, coriolis)
    sent = pack(owner.transpose(0, 2, 1), column, misfit, state, devices)
    got = lax.all_to_all(sent.reshape(devices, 1, WIRE * 128), ("tx", "ty"), split_axis=0, concat_axis=0, tiled=True)
    still, uv, frame = first_step(state, coefficients)
    ts, lists, corners, edges = first_records(got.reshape(devices * WIRE, 128), still, frame)
    x0 = swapped(edges[0], "tx", 0)
    x1 = swapped(edges[1], "tx", 1)
    y0 = swapped(edges[2], "ty", 0)
    y1 = swapped(edges[3], "ty", 1)
    forcing = second_records(lists)
    return last_step(ts, uv, coefficients, (x0, x1, y0, y1), frame, corners, forcing).reshape(FIELDS, LEV, CA, CB)


def solution(mesh):
    return jax.shard_map(
        local,
        mesh=mesh,
        in_specs=(
            P(None, None, "tx", "ty"),
            P(None, "tx", "ty"),
            P(None, "tx", "ty"),
            P(None, None, "tx", "ty"),
            P("tx", "ty"),
            P(None, None, ("tx", "ty")),
            P(None, ("tx", "ty"), None),
            P(None, ("tx", "ty")),
        ),
        out_specs=P(None, None, "tx", "ty"),
        check_vma=False,
    )
```
